512 devices in a mesh: dp: 128 (over z, y, core), mp: 4 (over x).
Axes of the slice: x: 4, y: 4, z: 16, core: 2. Of those that a mesh axis runs over, the one named last changes fastest.
Arguments:
- x_work: bfloat16 [49152, 1280], P('dp', 'mp'), may hold values from -14 to 14
- norm_gain: bfloat16 [1280], P('mp'), may hold values from 0.099609375 to 1.8984375
- w_qkv: bfloat16 [1280, 1920], P(None, 'mp'), may hold values from -0.2934839 to 0.2934839
- w_out: bfloat16 [640, 1280], P('mp'), may hold values from -0.9373467 to 0.9373467
- cot_owned: bfloat16 [90112, 1280], P('dp', 'mp'), may hold values from -10.5 to 10.5
- counts: int32 [128], replicated, may hold values from 1 to 11, as said below
Outputs:
- y_owned: bfloat16 [90112, 1280], P('dp', 'mp')
- x_grad: bfloat16 [49152, 1280], P('dp', 'mp')
- qkv_grad: float32 [1280, 1920], P(None, 'mp')
- out_grad: float32 [640, 1280], P('mp')
- gain_grad: float32 [1280], P('mp')
The draws below stay inside these ranges and needn't reach their ends.
Inputs may be any that keep to these rules, and one draw needn't show every extreme that they name: Live slots of an owner are its first counts[o] slots; with P[o] = starts[o] - o * 6, every P[o] lies in 0 .. 5 and P[0] = 0; the counts sum to 768.
All inputs are finite; a program needn't handle non-finite values.
Results may differ from the reference program's by a relative error of at most 0.0077.
Values may be sent and summed in bfloat16 or wider, within the bound.
No kernel may reach another device: no remote copies, remote signals or barrier semaphores. Data moves between devices by JAX's collectives and lax.ppermute only.
A program may use at most 64 MiB of HBM per device.

```python
import jax
import jax.numpy as jnp
from jax import lax

D = 1280
HEADS = 8
HD = 80
WIN = 64
W_DEV = 6
O_DEV = 11
NWIN = 768
ATT = 640
N_DP = 128


def routing_counts(key):
    key = jax.random.fold_in(key, 11)
    key_flow, key_place = jax.random.split(key, 2)
    flows = jax.random.randint(key_flow, (N_DP,), 0, W_DEV, dtype=jnp.int32)
    place = jax.random.randint(key_place, (), 0, N_DP - 2, dtype=jnp.int32)
    ranks = jnp.arange(N_DP, dtype=jnp.int32)
    flows = jnp.where(ranks == place - 1, 0, flows)
    flows = jnp.where(ranks == place, W_DEV - 1, flows)
    flows = jnp.where(ranks == place + 1, 0, flows)
    flows = jnp.where(ranks == N_DP - 1, 0, flows)
    earlier = jnp.concatenate([jnp.zeros((1,), jnp.int32), flows[:-1]])
    return (W_DEV + flows - earlier).astype(jnp.int32)


def feature_scale():
    position = jnp.arange(D, dtype=jnp.float32) / (D - 1) - 0.5
    return jnp.exp(jnp.log(3.0) * position)


def window_table(key):
    key = jax.random.fold_in(key, 23)
    key_shape, key_sign = jax.random.split(key, 2)
    window_rows = jnp.clip(jax.random.normal(key_shape, (NWIN, D), jnp.float32), -5.0, 5.0)
    window_rows = window_rows * feature_scale()[None, :]
    window_sign = (jax.random.randint(key_sign, (NWIN,), 0, 2, dtype=jnp.int32) * 2 - 1).astype(jnp.float32)
    return (window_rows, window_sign)


def value_part(key):
    key = jax.random.fold_in(key, 31)
    values = jnp.clip(jax.random.normal(key, (D, HEADS, HD), jnp.float32), -4.0, 4.0)
    band_width = D // HEADS
    feature_head = jnp.arange(D, dtype=jnp.int32) // band_width
    head_ids = jnp.arange(HEADS, dtype=jnp.int32)
    emphasis = jnp.where(feature_head[:, None] == head_ids[None, :], 5.0, 1.0)
    divisor = (24.0 / HEADS + 1.0) ** 0.5
    return values * emphasis[:, :, None] / divisor * D ** (-0.5)


def draw_counts(key, part):
    return routing_counts(key)


def draw_x_work(key, part):
    window_rows, window_sign = window_table(key)
    key = jax.random.fold_in(key, 5)
    jitter = jnp.clip(jax.random.normal(key, (NWIN, WIN, D), jnp.float32), -5.0, 5.0)
    inputs = window_rows[:, None, :] + jitter
    return inputs.reshape(NWIN * WIN, D).astype(jnp.bfloat16)


def draw_cot_owned(key, part):
    counts = routing_counts(key)
    window_rows, window_sign = window_table(key)
    key = jax.random.fold_in(key, 17)
    jitter = jnp.clip(jax.random.normal(key, (N_DP, O_DEV, WIN, D), jnp.float32), -5.0, 5.0)
    count_ends = jnp.cumsum(counts).astype(jnp.int32)
    starts = count_ends - counts
    slot_ids = jnp.arange(O_DEV, dtype=jnp.int32)
    order_ids = starts[:, None] + slot_ids[None, :]
    alive = slot_ids[None, :] < counts[:, None]
    target = jnp.clip(order_ids, 0, NWIN - 1).astype(jnp.int32)
    shared = (window_rows * window_sign[:, None])[target] * 0.9
    live_rows = shared[:, :, None, :] + 0.45 * jitter
    result = jnp.where(alive[:, :, None, None], live_rows, jitter)
    return result.reshape(N_DP * O_DEV * WIN, D).astype(jnp.bfloat16)


def draw_w_qkv(key, part):
    value_cols = value_part(key)
    key = jax.random.fold_in(key, 7)
    key_base = jax.random.fold_in(key, 0)
    paired = jnp.clip(jax.random.normal(key_base, (D, HEADS, 2, HD), jnp.float32), -6.0, 6.0) * D ** (-0.5)
    query_part = paired[:, :, 0:1]
    key_part = paired[:, :, 1:2]
    joined = jnp.concatenate([query_part, key_part, value_cols[:, :, None, :]], axis=2)
    return joined.reshape(D, 3 * HEADS * HD).astype(jnp.bfloat16)


def draw_w_out(key, part):
    value_cols = value_part(key)
    key = jax.random.fold_in(key, 13)
    jitter = jnp.clip(jax.random.normal(key, (ATT, D), jnp.float32), -5.0, 5.0)
    tied = value_cols.reshape(D, HEADS * HD).T
    return (3.0 * tied + 0.5 * jitter * ATT ** (-0.5)).astype(jnp.bfloat16)


def setup_inputs(seed: int = 0) -> dict:
    key_list = jax.random.split(jax.random.key(seed), 7)
    return {
        "x_work": draw_x_work(jax.random.fold_in(key_list[6], 71), 0),
        "norm_gain": jnp.clip(1.0 + 0.18 * jax.random.normal(key_list[1], (D,), jnp.float32), 0.099609375, 1.8984375).astype(jnp.bfloat16),
        "w_qkv": draw_w_qkv(jax.random.fold_in(key_list[6], 71), 0),
        "w_out": draw_w_out(jax.random.fold_in(key_list[6], 71), 0),
        "cot_owned": draw_cot_owned(jax.random.fold_in(key_list[6], 71), 0),
        "counts": draw_counts(jax.random.fold_in(key_list[6], 71), 0),
    }


epsilon = 1e-06

def split_heads(packed, window_count, heads_here):
    grid = packed.reshape(window_count, WIN, heads_here, 3, HD).astype(jnp.float32)
    return (grid[:, :, :, 0], grid[:, :, :, 1], grid[:, :, :, 2])

def reference(x_work, norm_gain, w_qkv, w_out, cot_owned, counts):
    row_count = x_work.shape[0]
    window_count = row_count // WIN
    x_float = x_work.astype(jnp.float32)
    inverse_rms = lax.rsqrt(lax.optimization_barrier(jnp.mean(x_float * x_float, axis=1, keepdims=True)) + epsilon)
    x_hat = x_float * inverse_rms
    gain_float = norm_gain.astype(jnp.float32)
    normed = (x_hat * gain_float).astype(jnp.bfloat16)
    packed = jnp.dot(normed, w_qkv, preferred_element_type=jnp.float32).astype(jnp.bfloat16)
    queries, key_heads, value_heads = split_heads(packed, window_count, HEADS)
    scores = jnp.einsum('wqhd,wkhd->whqk', queries, key_heads) * HD ** (-0.5)
    probabilities = jax.nn.softmax(scores, axis=-1)
    weights = lax.optimization_barrier(probabilities.astype(jnp.bfloat16)).astype(jnp.float32)
    mixed_heads = jnp.einsum('whqk,wkhd->wqhd', weights, value_heads).astype(jnp.bfloat16)
    mixed_heads = mixed_heads.reshape(row_count, HEADS * HD)
    branch = jnp.dot(mixed_heads, w_out, preferred_element_type=jnp.float32)
    y_work = (x_float + branch).astype(jnp.bfloat16)
    counts = counts.astype(jnp.int32)
    count_ends = jnp.cumsum(counts).astype(jnp.int32)
    starts = count_ends - counts
    slot_ids = jnp.arange(O_DEV, dtype=jnp.int32)
    order_ids = starts[:, None] + slot_ids[None, :]
    alive = slot_ids[None, :] < counts[:, None]
    target = jnp.clip(order_ids, 0, window_count - 1).astype(jnp.int32)
    y_windows = y_work.reshape(window_count, WIN, D)
    y_owned = jnp.where(alive[:, :, None, None], y_windows[target], jnp.zeros((), jnp.bfloat16))
    y_owned = y_owned.reshape(N_DP * O_DEV * WIN, D)
    wanted = jnp.arange(window_count, dtype=jnp.int32)
    owner_rank = lax.optimization_barrier(jnp.sum((count_ends[None, :] <= wanted[:, None]).astype(jnp.int32), axis=1))
    source = (owner_rank * O_DEV + wanted - starts[owner_rank]).astype(jnp.int32)
    cot_work = cot_owned.reshape(N_DP * O_DEV, WIN, D)[source].reshape(row_count, D)
    out_grad = jnp.dot(mixed_heads.T, cot_work, preferred_element_type=jnp.float32)
    grad_mixed = jnp.dot(cot_work, w_out.T, preferred_element_type=jnp.float32).astype(jnp.bfloat16)
    grad_mixed = lax.optimization_barrier(grad_mixed).astype(jnp.float32)
    grad_mixed = grad_mixed.reshape(window_count, WIN, HEADS, HD)
    grad_weights = jnp.einsum('wqhd,wkhd->whqk', grad_mixed, value_heads)
    grad_values = jnp.einsum('whqk,wqhd->wkhd', weights, grad_mixed)
    grad_scores = probabilities * (grad_weights - lax.optimization_barrier(jnp.sum(grad_weights * probabilities, axis=-1, keepdims=True))) * HD ** (-0.5)
    grad_query = jnp.einsum('whqk,wkhd->wqhd', grad_scores, key_heads)
    grad_keys = jnp.einsum('whqk,wqhd->wkhd', grad_scores, queries)
    grad_packed = jnp.stack([grad_query, grad_keys, grad_values], axis=3)
    grad_packed = grad_packed.reshape(row_count, 3 * HEADS * HD).astype(jnp.bfloat16)
    qkv_grad = jnp.dot(normed.T, grad_packed, preferred_element_type=jnp.float32)
    grad_normed = jnp.dot(grad_packed, w_qkv.T, preferred_element_type=jnp.float32)
    gain_grad = lax.optimization_barrier(jnp.sum(grad_normed * x_hat, axis=0))
    scaled = grad_normed * gain_float
    row_dot = lax.optimization_barrier(jnp.sum(scaled * x_hat, axis=1, keepdims=True)) / D
    x_grad = (cot_work.astype(jnp.float32) + inverse_rms * (scaled - x_hat * row_dot)).astype(jnp.bfloat16)
    return (y_owned, x_grad, qkv_grad, out_grad, gain_grad)
```

```python
import jax
import jax.numpy as jnp
from jax import lax
from jax.experimental import pallas as pl
from jax.experimental.pallas import tpu as pltpu
from jax.sharding import Mesh, PartitionSpec as P

HD = 80
WIN = 64
W_DEV = 6
epsilon = 1e-06

F32 = jnp.float32
BF16 = jnp.bfloat16
DP = ("zh", "zl", "y", "c")

FEAT = 1280
ROWS = 384
FX = 320
QKV = 480
ATT = 160
HEADS = 2
SLOTS = 704
PASS = 320
GROWS = 336

HALF = 25600
Y_LANES = 6400
Z_LANES = 1664
TILE = 128

VMEM = pl.BlockSpec(memory_space=pltpu.VMEM)


def call(kernel, out_shapes, scratch=(), vmem_mib=24, flops=1000000):
    return pl.pallas_call(
        kernel,
        out_shape=out_shapes,
        scratch_shapes=list(scratch),
        compiler_params=pltpu.CompilerParams(vmem_limit_bytes=vmem_mib * 1024 * 1024),
        cost_estimate=pl.CostEstimate(flops=flops, bytes_accessed=1000000, transcendentals=0),
    )


def struct(shape, dtype):
    return jax.ShapeDtypeStruct(shape, dtype)


def drift_of(counts_row, rank):
    owners = lax.broadcasted_iota(jnp.int32, counts_row.shape, 1)
    before = jnp.sum(jnp.where(owners < rank, counts_row, 0), axis=1, keepdims=True)
    return before - rank * W_DEV


def one_hot(rows, cols, shift):
    r = lax.broadcasted_iota(jnp.int32, (rows, cols), 0)
    c = lax.broadcasted_iota(jnp.int32, (rows, cols), 1)
    return jnp.where(r == c + shift, 1.0, 0.0).astype(BF16)


def dot(a, b, dims):
    return lax.dot_general(a, b, ((dims[:1], dims[1:]), ((), ())), preferred_element_type=F32)


def route_send(counts_ref, cot_ref, send_ref):
    rank = lax.axis_index(DP)
    drift = drift_of(counts_ref[...], rank)
    pick = one_hot(SLOTS, PASS, (W_DEV - drift) * WIN)
    send_ref[...] = dot(cot_ref[...], pick, (1, 0)).astype(BF16)


def route_in(counts_ref, gain_ref, cot_ref, got_ref, out_ref):
    rank = lax.axis_index(DP)
    drift = drift_of(counts_ref[...], rank) * WIN
    own = dot(cot_ref[:, :ROWS], one_hot(ROWS, ROWS, -drift), (1, 0))
    col = lax.broadcasted_iota(jnp.int32, (PASS, ROWS), 1)
    row = lax.broadcasted_iota(jnp.int32, (PASS, ROWS), 0)
    near = jnp.where((row == col) & (col < drift), 1.0, 0.0).astype(BF16)
    out_ref[:FX, :] = (own + dot(got_ref[...], near, (1, 0))).astype(BF16)
    out_ref[FX:, :] = jnp.zeros((GROWS - FX, ROWS), BF16)
    out_ref[FX:, :FX] = jnp.broadcast_to(gain_ref[...], (GROWS - FX, FX))


def block(x_ref, g_ref, wq_ref, wo_ref, mp_ref, send_ref, keep_ref, gcol, nrm, gt, pk, gm, mx, gp, part, dsum):
    core = lax.axis_index("c")
    r_i = lax.broadcasted_iota(jnp.int32, (FX, ROWS), 0)
    c_i = lax.broadcasted_iota(jnp.int32, (FX, ROWS), 1)
    for j in range(4):
        gt[FX * j:FX * (j + 1), :] = g_ref[j, :FX, :]
        row = g_ref[j, FX:GROWS, :].astype(F32)[:1, :]
        gcol[FX * j:FX * (j + 1), :] = jnp.sum(jnp.where(r_i == c_i, row, 0.0), axis=1, keepdims=True)
    total = jnp.zeros((8, ROWS), F32)
    for i in range(16):
        x = x_ref[80 * i:80 * (i + 1), :].astype(F32)
        total += jnp.sum((x * x).reshape(10, 8, ROWS), axis=0)
    rms = lax.rsqrt(jnp.sum(total, axis=0, keepdims=True) / FEAT + epsilon)
    for i in range(16):
        s = slice(80 * i, 80 * (i + 1))
        nrm[s, :] = ((x_ref[s, :].astype(F32) * rms) * gcol[s, :]).astype(BF16)
    pk[...] = dot(wq_ref[...], nrm[...], (1, 0)).astype(BF16)
    gm[...] = dot(wo_ref[...], gt[...], (1, 0)).astype(BF16)
    qi = lax.broadcasted_iota(jnp.int32, (128, 128), 0)
    ki = lax.broadcasted_iota(jnp.int32, (128, 128), 1)
    same = (qi < WIN) == (ki < WIN)
    scale = HD ** (-0.5)
    for h in range(HEADS):
        for p in range(3):
            c = slice(128 * p, 128 * (p + 1))
            b = 3 * HD * h
            q, k, v = (pk[b + HD * t:b + HD * (t + 1), c] for t in range(3))
            g = gm[HD * h:HD * (h + 1), c]
            scores = jnp.where(same, dot(q, k, (0, 0)) * scale, -jnp.inf)
            e = jnp.exp(scores - jnp.max(scores, axis=1, keepdims=True))
            probs = e / jnp.sum(e, axis=1, keepdims=True)
            weights = probs.astype(BF16)
            mx[HD * h:HD * (h + 1), c] = dot(v, weights, (1, 1)).astype(BF16)
            dw = dot(g, v, (0, 0))
            ds = probs * (dw - jnp.sum(dw * probs, axis=1, keepdims=True)) * scale
            ds = ds.astype(BF16)
            gp[b:b + HD, c] = dot(k, ds, (1, 1)).astype(BF16)
            gp[b + HD:b + 2 * HD, c] = dot(q, ds, (1, 0)).astype(BF16)
            gp[b + 2 * HD:b + 3 * HD, c] = dot(g, weights, (1, 0)).astype(BF16)
    dsum[:QKV, :] = dot(gp[...], nrm[...], (1, 1))
    dsum[QKV:, :] = dot(mx[...], gt[...], (1, 1))
    for i in range(20):
        c = slice(FEAT * i, FEAT * (i + 1))
        keep_ref[:, c] = dsum[pl.ds(pl.multiple_of(core * 320 + 16 * i, 16), 16), :]
        send_ref[:, c] = dsum[pl.ds(pl.multiple_of((1 - core) * 320 + 16 * i, 16), 16), :].astype(BF16)
    part[...] = dot(wo_ref[...], mx[...], (0, 0))
    for i in range(20):
        j, o = divmod(64 * i, FX)
        mp_ref[j, o:o + 64, :] = part[64 * i:64 * (i + 1), :].astype(BF16)
    part[...] = dot(wq_ref[...], gp[...], (0, 0))
    row_dot = jnp.zeros((8, ROWS), F32)
    tile_row = lax.broadcasted_iota(jnp.int32, (16, TILE), 0)
    gain_tile = jnp.zeros((16, TILE), F32)
    for i in range(10):
        s = slice(128 * i, 128 * (i + 1))
        t = part[s, :] * (x_ref[s, :].astype(F32) * rms)
        row_dot += jnp.sum((t * gcol[s, :]).reshape(16, 8, ROWS), axis=0)
        lanes = t[:, :128] + t[:, 128:256] + t[:, 256:]
        line = jnp.sum(lanes.T, axis=0, keepdims=True)
        gain_tile = jnp.where(tile_row == i, line, gain_tile)
    gain_tile = gain_tile.astype(BF16)
    send_ref[:, HALF:] = gain_tile
    keep_ref[:, HALF:] = gain_tile.astype(F32)
    mean = jnp.sum(row_dot, axis=0, keepdims=True) / FEAT
    for i in range(20):
        s = slice(64 * i, 64 * (i + 1))
        j, o = divmod(64 * i, FX)
        z = rms * (part[s, :] * gcol[s, :] - (x_ref[s, :].astype(F32) * rms) * mean)
        mp_ref[j, FX + o:FX + o + 64, :] = z.astype(BF16)


def core_sum(keep_ref, got_ref, out_ref):
    gain = (keep_ref[:, HALF:] + got_ref[:, HALF:].astype(F32)).astype(BF16)
    for b in range(4):
        s = slice(Y_LANES * b, Y_LANES * (b + 1))
        out_ref[b, :, :Y_LANES] = (keep_ref[:, s] + got_ref[:, s].astype(F32)).astype(BF16)
        out_ref[b, :, Y_LANES:] = gain


def sum_of_four(ref, s):
    a, b, c, d = (ref[i, :, s].astype(F32) for i in range(4))
    return (a + b) + (c + d)


def y_sum(got_ref, out_ref):
    gain = sum_of_four(got_ref, slice(Y_LANES, Y_LANES + TILE)).astype(BF16)
    for b in range(4):
        lo, hi = Z_LANES * b, min(Z_LANES * (b + 1), Y_LANES)
        out_ref[b, :, :hi - lo] = sum_of_four(got_ref, slice(lo, hi)).astype(BF16)
        if hi - lo < Z_LANES:
            out_ref[b, :, hi - lo:Z_LANES] = jnp.zeros((16, Z_LANES - (hi - lo)), BF16)
        out_ref[b, :, Z_LANES:] = gain


def zl_sum(got_ref, out_ref):
    out_ref[...] = sum_of_four(got_ref, slice(None)).astype(BF16)


def zh_sum(got_ref, out_ref, gain_ref):
    out_ref[...] = sum_of_four(got_ref, slice(0, Z_LANES)).astype(BF16)
    gain_ref[...] = sum_of_four(got_ref, slice(Z_LANES, Z_LANES + TILE))


def z_pack(got_ref, out_ref):
    for b in range(4):
        lo, hi = Z_LANES * b, min(Z_LANES * (b + 1), Y_LANES)
        out_ref[:, lo:hi] = got_ref[b, :, :hi - lo]


def weight_out(own_ref, other_ref, qkv_ref, out_ref):
    core = lax.axis_index("c")

    def rows(first, second):
        for i in range(40):
            ref = first if i < 20 else second
            b, o = divmod(i % 20, 5)
            tile = ref[b, :, FEAT * o:FEAT * (o + 1)].astype(F32)
            if i < 30:
                qkv_ref[16 * i:16 * (i + 1), :] = tile
            else:
                out_ref[16 * (i - 30):16 * (i - 29), :] = tile

    @pl.when(core == 0)
    def _():
        rows(own_ref, other_ref)

    @pl.when(core == 1)
    def _():
        rows(other_ref, own_ref)


def gain_out(a_ref, b_ref, c_ref, d_ref, out_ref):
    mp = lax.axis_index("x")
    tile = (a_ref[...] + b_ref[...]) + (c_ref[...] + d_ref[...])
    line = jnp.concatenate([tile[i:i + 1, :] for i in range(10)], axis=1)
    out = jnp.zeros((1, FX), F32)
    for j in range(4):
        out = jnp.where(mp == j, line[:, FX * j:FX * (j + 1)], out)
    out_ref[...] = out


def heads_sum(got_ref, x_ref, cot_ref, y_ref, send_ref, grad_ref):
    for i in range(5):
        s = slice(64 * i, 64 * (i + 1))
        t = slice(FX + 64 * i, FX + 64 * (i + 1))
        a, b, c, d = (got_ref[j, s, :].astype(F32) for j in range(4))
        y = (x_ref[s, :].astype(F32) + ((a + b) + (c + d))).astype(BF16)
        y_ref[s, :] = y
        send_ref[s, :] = y[:, :PASS]
        a, b, c, d = (got_ref[j, t, :].astype(F32) for j in range(4))
        grad_ref[s, :] = (cot_ref[s, :].astype(F32) + ((a + b) + (c + d))).astype(BF16)


def route_out(counts_ref, y_ref, got_ref, out_ref):
    rank = lax.axis_index(DP)
    counts = counts_ref[...]
    owners = lax.broadcasted_iota(jnp.int32, counts.shape, 1)
    live = jnp.sum(jnp.where(owners == rank, counts, 0), axis=1, keepdims=True) * WIN
    drift = drift_of(counts, rank) * WIN
    kept = W_DEV * WIN - drift
    r = lax.broadcasted_iota(jnp.int32, (ROWS, SLOTS), 0)
    c = lax.broadcasted_iota(jnp.int32, (ROWS, SLOTS), 1)
    own = jnp.where((r == c + drift) & (c < live), 1.0, 0.0).astype(BF16)
    r, c = r[:PASS], c[:PASS]
    far = jnp.where((r == c - kept) & (c < live), 1.0, 0.0).astype(BF16)
    out_ref[...] = (dot(y_ref[...], own, (1, 0)) + dot(got_ref[...], far, (1, 0))).astype(BF16)


def shards(x_work, norm_gain, w_qkv, w_out, cot_owned, counts):
    xt, cot, wq = x_work.T, cot_owned.T, w_qkv.T
    counts = counts.reshape(1, -1)
    gain = norm_gain.reshape(1, -1)
    up = [(i, i + 1) for i in range(127)]
    down = [(i + 1, i) for i in range(127)]
    cores = [(0, 1), (1, 0)]

    send = call(route_send, struct((FX, PASS), BF16))(counts, cot)
    got = lax.ppermute(send, DP, up)
    x_full = lax.all_gather(xt, "x", axis=0, tiled=True)
    cot_work = call(route_in, struct((GROWS, ROWS), BF16))(counts, gain, cot, got)
    g_full = lax.all_gather(cot_work, "x", axis=0)

    heads, send, keep = call(
        block,
        (
            struct((4, 2 * FX, ROWS), BF16),
            struct((16, HALF + TILE), BF16),
            struct((16, HALF + TILE), F32),
        ),
        scratch=(
            pltpu.VMEM((FEAT, 1), F32),
            pltpu.VMEM((FEAT, ROWS), BF16),
            pltpu.VMEM((FEAT, ROWS), BF16),
            pltpu.VMEM((QKV, ROWS), BF16),
            pltpu.VMEM((ATT, ROWS), BF16),
            pltpu.VMEM((ATT, ROWS), BF16),
            pltpu.VMEM((QKV, ROWS), BF16),
            pltpu.VMEM((FEAT, ROWS), F32),
            pltpu.VMEM((QKV + ATT, FEAT), F32),
        ),
        vmem_mib=48,
        flops=2000000000,
    )(x_full, g_full, wq, w_out)

    heads = lax.all_to_all(heads, "x", 0, 0)

    got = lax.ppermute(send, "c", cores)
    parts = call(core_sum, struct((4, 16, Y_LANES + TILE), BF16))(keep, got)
    parts = lax.all_to_all(parts, "y", 0, 0)
    parts = call(y_sum, struct((4, 16, Z_LANES + TILE), BF16))(parts)
    parts = lax.all_to_all(parts, "zl", 0, 0)
    part = call(zl_sum, struct((16, Z_LANES + TILE), BF16))(parts)
    parts = lax.all_gather(part, "zh", axis=0)
    part, gain_own = call(zh_sum, (struct((16, Z_LANES), BF16), struct((16, TILE), F32)))(parts)
    gain_got = [lax.ppermute(gain_own, "x", [(i, (i + k) % 4) for i in range(4)]) for k in (1, 2, 3)]
    parts = lax.all_gather(part, "zl", axis=0)
    part = call(z_pack, struct((16, Y_LANES), BF16))(parts)
    own = lax.all_gather(part, "y", axis=0)
    other = lax.ppermute(own, "c", cores)
    qkv_grad, out_grad = call(weight_out, (struct((QKV, FEAT), F32), struct((ATT, FEAT), F32)))(own, other)
    gain_grad = call(gain_out, struct((1, FX), F32))(gain_own, *gain_got)

    y_work, send, x_grad = call(
        heads_sum,
        (struct((FX, ROWS), BF16), struct((FX, PASS), BF16), struct((FX, ROWS), BF16)),
    )(heads, xt, cot_work)
    got = lax.ppermute(send, DP, down)
    y_owned = call(route_out, struct((FX, SLOTS), BF16))(counts, y_work, got)
    return (y_owned.T, x_grad.T, qkv_grad.T, out_grad, gain_grad.reshape(FX))


def solution(mesh):
    fine = Mesh(mesh.devices.reshape(4, 4, 4, 2, 4), DP + ("x",))
    return jax.shard_map(
        shards,
        mesh=fine,
        in_specs=(P(DP, "x"), P("x"), P(None, "x"), P("x", None), P(DP, "x"), P()),
        out_specs=(P(DP, "x"), P(DP, "x"), P(None, "x"), P("x", None), P("x")),
        check_vma=False,
    )
```

```python
import jax
import jax.numpy as jnp
from jax import lax
from jax.experimental import pallas as pl
from jax.experimental.pallas import tpu as pltpu
from jax.sharding import Mesh, PartitionSpec as P

HD = 80
WIN = 64
W_DEV = 6
epsilon = 1e-06

F32 = jnp.float32
BF16 = jnp.bfloat16
DP = ("zh", "zl", "y", "c")

FEAT = 1280
ROWS = 384
FX = 320
QKV = 480
ATT = 160
HEADS = 2
SLOTS = 704
PASS = 320
GROWS = 336

HALF = 25600
Y_LANES = 6400
Z_LANES = 1664
TILE = 128

VMEM = pl.BlockSpec(memory_space=pltpu.VMEM)
ANY = pl.BlockSpec(memory_space=pl.ANY)
HBM = pl.BlockSpec(memory_space=pltpu.HBM)


def call(kernel, out_shapes, ins=None, outs=None, aliases=None, scratch=(), vmem_mib=24, flops=1000000):
    specs = {}
    if ins is not None:
        specs["in_specs"] = ins
    if outs is not None:
        specs["out_specs"] = outs
    return pl.pallas_call(
        kernel,
        out_shape=out_shapes,
        scratch_shapes=list(scratch),
        input_output_aliases=aliases or {},
        compiler_params=pltpu.CompilerParams(vmem_limit_bytes=vmem_mib * 1024 * 1024),
        cost_estimate=pl.CostEstimate(flops=flops, bytes_accessed=1000000, transcendentals=0),
        **specs,
    )


def struct(shape, dtype):
    return jax.ShapeDtypeStruct(shape, dtype)


def drift_of(counts_row, rank):
    owners = lax.broadcasted_iota(jnp.int32, counts_row.shape, 1)
    before = jnp.sum(jnp.where(owners < rank, counts_row, 0), axis=1, keepdims=True)
    return before - rank * W_DEV


def one_hot(rows, cols, shift):
    r = lax.broadcasted_iota(jnp.int32, (rows, cols), 0)
    c = lax.broadcasted_iota(jnp.int32, (rows, cols), 1)
    return jnp.where(r == c + shift, 1.0, 0.0).astype(BF16)


def dot(a, b, dims):
    return lax.dot_general(a, b, ((dims[:1], dims[1:]), ((), ())), preferred_element_type=F32)


def enter(counts_hbm, cot_hbm, send_ref, counts, cot, sems):
    copies = [
        pltpu.make_async_copy(counts_hbm, counts, sems.at[0]),
        pltpu.make_async_copy(cot_hbm, cot, sems.at[1]),
    ]
    for copy in copies:
        copy.start()
    for copy in copies:
        copy.wait()
    drift = drift_of(counts[...], lax.axis_index(DP))
    pick = one_hot(SLOTS, PASS, (W_DEV - drift) * WIN)
    send_ref[...] = dot(cot[...], pick, (1, 0)).astype(BF16)


def route_in(counts_ref, gain_ref, cot_ref, got_ref, out_ref):
    drift = drift_of(counts_ref[...], lax.axis_index(DP)) * WIN
    own = dot(cot_ref[:, :ROWS], one_hot(ROWS, ROWS, -drift), (1, 0))
    col = lax.broadcasted_iota(jnp.int32, (PASS, ROWS), 1)
    row = lax.broadcasted_iota(jnp.int32, (PASS, ROWS), 0)
    near = jnp.where((row == col) & (col < drift), 1.0, 0.0).astype(BF16)
    out_ref[:FX, :] = (own + dot(got_ref[...], near, (1, 0))).astype(BF16)
    out_ref[FX:, :] = jnp.zeros((GROWS - FX, ROWS), BF16)
    out_ref[FX:, :FX] = jnp.broadcast_to(gain_ref[...], (GROWS - FX, FX))


def x_rows(x_ref, i):
    return x_ref[80 * i:80 * (i + 1), :]


def pairs():
    return [(3 * h + p, h, slice(128 * p, 128 * (p + 1)), 3 * HD * h) for h in range(HEADS) for p in range(3)]


def block(x_ref, g_ref, wq_ref, wo_ref, send_ref, keep_ref, gp_ref, mx_ref, gcol_ref, rms_ref, gt, nrm, pk, gm, dsum):
    core = lax.axis_index("c")
    r_i = lax.broadcasted_iota(jnp.int32, (FX, ROWS), 0)
    c_i = lax.broadcasted_iota(jnp.int32, (FX, ROWS), 1)
    total = jnp.zeros((8, ROWS), F32)
    for i in range(16):
        x = x_rows(x_ref, i).astype(F32)
        total += jnp.sum((x * x).reshape(10, 8, ROWS), axis=0)
    rms = lax.rsqrt(jnp.sum(total, axis=0, keepdims=True) / FEAT + epsilon)
    rms_ref[...] = rms
    for j in range(4):
        gt[FX * j:FX * (j + 1), :] = g_ref[j, :FX, :]
        row = g_ref[j, FX:, :].astype(F32)[:1, :]
        gcol_ref[FX * j:FX * (j + 1), :] = jnp.sum(jnp.where(r_i == c_i, row, 0.0), axis=1, keepdims=True)
    for i in range(16):
        s = slice(80 * i, 80 * (i + 1))
        nrm[s, :] = ((x_rows(x_ref, i).astype(F32) * rms) * gcol_ref[s, :]).astype(BF16)
    pk[...] = dot(wq_ref[...], nrm[...], (1, 0)).astype(BF16)
    gm[...] = dot(wo_ref[...], gt[...], (1, 0)).astype(BF16)
    qi = lax.broadcasted_iota(jnp.int32, (128, 128), 0)
    ki = lax.broadcasted_iota(jnp.int32, (128, 128), 1)
    same = (qi < WIN) == (ki < WIN)
    scores = [
        jnp.where(same, dot(pk[b:b + HD, c], pk[b + HD:b + 2 * HD, c], (0, 0)) * HD ** (-0.5), -jnp.inf)
        for _, _, c, b in pairs()
    ]
    dws = [dot(gm[HD * h:HD * (h + 1), c], pk[b + 2 * HD:b + 3 * HD, c], (0, 0)) for _, h, c, b in pairs()]
    exps = [jnp.exp(s - jnp.max(s, axis=1, keepdims=True)) for s in scores]
    probs = [e / jnp.sum(e, axis=1, keepdims=True) for e in exps]
    weights = [p.astype(BF16) for p in probs]
    dss = [
        (p * (dw - jnp.sum(dw * p, axis=1, keepdims=True)) * HD ** (-0.5)).astype(BF16)
        for p, dw in zip(probs, dws)
    ]
    for n, h, c, b in pairs():
        mx_ref[HD * h:HD * (h + 1), c] = dot(pk[b + 2 * HD:b + 3 * HD, c], weights[n], (1, 1)).astype(BF16)
        gp_ref[b:b + HD, c] = dot(pk[b + HD:b + 2 * HD, c], dss[n], (1, 1)).astype(BF16)
        gp_ref[b + HD:b + 2 * HD, c] = dot(pk[b:b + HD, c], dss[n], (1, 0)).astype(BF16)
        gp_ref[b + 2 * HD:b + 3 * HD, c] = dot(gm[HD * h:HD * (h + 1), c], weights[n], (1, 0)).astype(BF16)
    dsum[:QKV, :] = dot(gp_ref[...], nrm[...], (1, 1))
    dsum[QKV:, :] = dot(mx_ref[...], gt[...], (1, 1))
    for i in range(20):
        c = slice(FEAT * i, FEAT * (i + 1))
        keep_ref[:, c] = dsum[pl.ds(pl.multiple_of(core * 320 + 16 * i, 16), 16), :]
        send_ref[:, c] = dsum[pl.ds(pl.multiple_of((1 - core) * 320 + 16 * i, 16), 16), :].astype(BF16)
    total = jnp.zeros((8, FEAT), F32)
    for i in range(30):
        s = slice(16 * i, 16 * (i + 1))
        total += jnp.sum((wq_ref[s, :].astype(F32) * dsum[s, :]).reshape(2, 8, FEAT), axis=0)
    line = jnp.sum(total, axis=0, keepdims=True)
    tile_row = lax.broadcasted_iota(jnp.int32, (16, TILE), 0)
    tile = jnp.zeros((16, TILE), F32)
    for i in range(10):
        tile = jnp.where(tile_row == i, line[:, TILE * i:TILE * (i + 1)], tile)
    tile = tile.astype(BF16)
    send_ref[:, HALF:] = tile
    keep_ref[:, HALF:] = tile.astype(F32)


def head_shares(gp_ref, mx_ref, x_ref, wq_ref, wo_ref, gcol_ref, rms_ref, heads_ref, part, out, sems):
    rms = rms_ref[...]
    part[...] = dot(wo_ref[...], mx_ref[...], (0, 0))
    for j in range(4):
        out[j, :FX, :] = part[FX * j:FX * (j + 1), :].astype(BF16)
    part[...] = dot(wq_ref[...], gp_ref[...], (0, 0))
    row_dot = jnp.zeros((8, ROWS), F32)
    for i in range(16):
        s = slice(80 * i, 80 * (i + 1))
        x = x_rows(x_ref, i).astype(F32)
        row_dot += jnp.sum(((part[s, :] * gcol_ref[s, :]) * (x * rms)).reshape(10, 8, ROWS), axis=0)
    mean = jnp.sum(row_dot, axis=0, keepdims=True) / FEAT
    copies = []
    for j in range(4):
        for i in range(4):
            s = slice(FX * j + 80 * i, FX * j + 80 * (i + 1))
            x = x_rows(x_ref, 4 * j + i).astype(F32)
            z = rms * (part[s, :] * gcol_ref[s, :] - (x * rms) * mean)
            out[j, FX + 80 * i:FX + 80 * (i + 1), :] = z.astype(BF16)
        copies.append(pltpu.make_async_copy(out.at[j], heads_ref.at[j, pl.ds(0, 2 * FX)], sems.at[j]))
        copies[j].start()
    for copy in copies:
        copy.wait()


def core_sum(keep_ref, got_ref, heads_ref, out_ref):
    gain = (keep_ref[:, HALF:] + got_ref[:, HALF:].astype(F32)).astype(BF16)
    for b in range(4):
        s = slice(Y_LANES * b, Y_LANES * (b + 1))
        out_ref[b, :, :Y_LANES] = (keep_ref[:, s] + got_ref[:, s].astype(F32)).astype(BF16)
        out_ref[b, :, Y_LANES:] = gain


def sum_of_four(ref, s):
    a, b, c, d = (ref[i, :, s].astype(F32) for i in range(4))
    return (a + b) + (c + d)


def y_sum(got_ref, out_ref):
    gain = sum_of_four(got_ref, slice(Y_LANES, Y_LANES + TILE)).astype(BF16)
    for b in range(4):
        lo, hi = Z_LANES * b, min(Z_LANES * (b + 1), Y_LANES)
        out_ref[b, :, :hi - lo] = sum_of_four(got_ref, slice(lo, hi)).astype(BF16)
        if hi - lo < Z_LANES:
            out_ref[b, :, hi - lo:Z_LANES] = jnp.zeros((16, Z_LANES - (hi - lo)), BF16)
        out_ref[b, :, Z_LANES:] = gain


def zl_sum(got_ref, out_ref):
    out_ref[...] = sum_of_four(got_ref, slice(None)).astype(BF16)


def pair_sum(own_ref, got_ref, out_ref):
    out_ref[...] = (own_ref[...].astype(F32) + got_ref[...].astype(F32)).astype(BF16)


def zh_sum(own_ref, got_ref, heads_in, out_ref, heads_ref, lines, sems):
    total = own_ref[...].astype(F32) + got_ref[...].astype(F32)
    out_ref[...] = total[:, :Z_LANES].astype(BF16)
    tile = total[:, Z_LANES:]
    line = jnp.concatenate([tile[i:i + 1, :] for i in range(10)], axis=1)
    row = lax.broadcasted_iota(jnp.int32, (16, FX), 0)
    copies = []
    for j in range(4):
        chunk = line[:, FX * j:FX * (j + 1)]
        high = chunk.astype(BF16).astype(F32)
        lines[j] = jnp.zeros((16, ROWS), BF16)
        lines[j, :, :FX] = jnp.where(row == 0, high, jnp.where(row == 1, chunk - high, 0.0)).astype(BF16)
        copies.append(pltpu.make_async_copy(lines.at[j], heads_ref.at[j, pl.ds(2 * FX, 16)], sems.at[j]))
        copies[j].start()
    for copy in copies:
        copy.wait()


def z_pack(got_ref, out_ref):
    for b in range(4):
        lo, hi = Z_LANES * b, min(Z_LANES * (b + 1), Y_LANES)
        out_ref[:, lo:hi] = got_ref[b, :, :hi - lo]


def weight_rows(ref, half, qkv_ref, out_ref, buf, sems):
    for b in range(4):
        for o in range(5):
            i = 5 * b + o
            buf[16 * i:16 * (i + 1), :] = ref[b, :, FEAT * o:FEAT * (o + 1)].astype(F32)
        chunk = buf.at[pl.ds(80 * b, 80)]

        @pl.when(half == 0)
        def _():
            pltpu.make_async_copy(chunk, qkv_ref.at[pl.ds(80 * b, 80)], sems.at[b]).start()

        @pl.when(half == 1)
        def _():
            target = qkv_ref.at[pl.ds(320 + 80 * b, 80)] if b < 2 else out_ref.at[pl.ds(80 * (b - 2), 80)]
            pltpu.make_async_copy(chunk, target, sems.at[b]).start()

    for b in range(4):
        chunk = buf.at[pl.ds(80 * b, 80)]
        pltpu.make_async_copy(chunk, qkv_ref.at[pl.ds(0, 80)], sems.at[b]).wait()


def weight_own(ref, qkv_ref, out_ref, buf, sems):
    weight_rows(ref, lax.axis_index("c"), qkv_ref, out_ref, buf, sems)


def weight_other(ref, qkv_in, out_in, qkv_ref, out_ref, buf, sems):
    weight_rows(ref, 1 - lax.axis_index("c"), qkv_ref, out_ref, buf, sems)


def heads_sum(got_ref, x_ref, cot_ref, gain_ref, y_ref, send_ref, grad_ref, gain_grad_ref):
    for i in range(5):
        s = slice(64 * i, 64 * (i + 1))
        t = slice(FX + 64 * i, FX + 64 * (i + 1))
        a, b, c, d = (got_ref[j, s, :].astype(F32) for j in range(4))
        y = (x_ref[s, :].astype(F32) + ((a + b) + (c + d))).astype(BF16)
        y_ref[s, :] = y
        send_ref[s, :] = y[:, :PASS]
        a, b, c, d = (got_ref[j, t, :].astype(F32) for j in range(4))
        grad_ref[s, :] = (cot_ref[s, :].astype(F32) + ((a + b) + (c + d))).astype(BF16)
    a, b, c, d = (got_ref[j, 2 * FX:, :].astype(F32) for j in range(4))
    line = jnp.sum((a + b) + (c + d), axis=0, keepdims=True)
    gain_grad_ref[...] = (line[:, :FX] / gain_ref[...].astype(F32)).reshape(FX)


def route_out(counts_ref, y_ref, got_ref, out_ref):
    rank = lax.axis_index(DP)
    counts = counts_ref[...]
    owners = lax.broadcasted_iota(jnp.int32, counts.shape, 1)
    live = jnp.sum(jnp.where(owners == rank, counts, 0), axis=1, keepdims=True) * WIN
    drift = drift_of(counts, rank) * WIN
    kept = W_DEV * WIN - drift
    r = lax.broadcasted_iota(jnp.int32, (ROWS, SLOTS), 0)
    c = lax.broadcasted_iota(jnp.int32, (ROWS, SLOTS), 1)
    own = jnp.where((r == c + drift) & (c < live), 1.0, 0.0).astype(BF16)
    r, c = r[:PASS], c[:PASS]
    far = jnp.where((r == c - kept) & (c < live), 1.0, 0.0).astype(BF16)
    out_ref[...] = (dot(y_ref[...], own, (1, 0)) + dot(got_ref[...], far, (1, 0))).astype(BF16)


def shards(x_work, norm_gain, w_qkv, w_out, cot_owned, counts):
    xt, cot, wq = x_work.T, cot_owned.T, w_qkv.T
    counts = counts.reshape(1, -1)
    gain = norm_gain.reshape(1, -1)
    up = [(i, i + 1) for i in range(127)]
    down = [(i + 1, i) for i in range(127)]
    cores = [(0, 1), (1, 0)]

    send = call(
        enter,
        struct((FX, PASS), BF16),
        ins=(HBM, HBM),
        scratch=(pltpu.VMEM((1, 128), jnp.int32), pltpu.VMEM((FX, SLOTS), BF16), pltpu.SemaphoreType.DMA((2,))),
    )(counts, cot)
    got = lax.ppermute(send, DP, up)
    x_full = lax.all_gather(xt, "x", axis=0, tiled=True)
    cot_work = call(route_in, struct((GROWS, ROWS), BF16))(counts, gain, cot, got)
    g_full = lax.all_gather(cot_work, "x", axis=0)

    send, keep, gp, mx, gcol, rms = call(
        block,
        (
            struct((16, HALF + TILE), BF16),
            struct((16, HALF + TILE), F32),
            struct((QKV, ROWS), BF16),
            struct((ATT, ROWS), BF16),
            struct((FEAT, 1), F32),
            struct((1, ROWS), F32),
        ),
        scratch=(
            pltpu.VMEM((FEAT, ROWS), BF16),
            pltpu.VMEM((FEAT, ROWS), BF16),
            pltpu.VMEM((QKV, ROWS), BF16),
            pltpu.VMEM((ATT, ROWS), BF16),
            pltpu.VMEM((QKV + ATT, FEAT), F32),
        ),
        vmem_mib=40,
        flops=1500000000,
    )(x_full, g_full, wq, w_out)

    got = lax.ppermute(send, "c", cores)
    heads_shape = struct((4, 2 * FX + 16, ROWS), BF16)
    heads = call(
        head_shares,
        heads_shape,
        outs=HBM,
        scratch=(
            pltpu.VMEM((FEAT, ROWS), F32),
            pltpu.VMEM((4, 2 * FX, ROWS), BF16),
            pltpu.SemaphoreType.DMA((4,)),
        ),
        vmem_mib=40,
        flops=700000000,
    )(gp, mx, x_full, wq, w_out, gcol, rms)

    parts = call(core_sum, struct((4, 16, Y_LANES + TILE), BF16), ins=(VMEM, VMEM, HBM))(keep, got, heads)
    parts = lax.all_to_all(parts, "y", 0, 0)
    parts = call(y_sum, struct((4, 16, Z_LANES + TILE), BF16))(parts)
    parts = lax.all_to_all(parts, "zl", 0, 0)
    part = call(zl_sum, struct((16, Z_LANES + TILE), BF16))(parts)
    got = lax.ppermute(part, "zh", [(0, 1), (1, 0), (2, 3), (3, 2)])
    part = call(pair_sum, struct((16, Z_LANES + TILE), BF16))(part, got)
    got = lax.ppermute(part, "zh", [(1, 2), (2, 1), (3, 0), (0, 3)])
    part, heads = call(
        zh_sum,
        (struct((16, Z_LANES), BF16), heads_shape),
        ins=(VMEM, VMEM, HBM),
        outs=(VMEM, HBM),
        aliases={2: 1},
        scratch=(pltpu.VMEM((4, 16, ROWS), BF16), pltpu.SemaphoreType.DMA((4,))),
    )(part, got, heads)
    heads = lax.all_to_all(heads, "x", 0, 0)
    parts = lax.all_gather(part, "zl", axis=0)
    part = call(z_pack, struct((16, Y_LANES), BF16))(parts)
    own = lax.all_gather(part, "y", axis=0)
    other = lax.ppermute(own, "c", cores)
    weight_shapes = (struct((QKV, FEAT), F32), struct((ATT, FEAT), F32))
    weight_scratch = (pltpu.VMEM((320, FEAT), F32), pltpu.SemaphoreType.DMA((4,)))
    weights = call(weight_own, weight_shapes, outs=(ANY, ANY), scratch=weight_scratch)(own)
    qkv_grad, out_grad = call(
        weight_other,
        weight_shapes,
        ins=(VMEM, ANY, ANY),
        outs=(ANY, ANY),
        aliases={1: 0, 2: 1},
        scratch=weight_scratch,
    )(other, *weights)

    y_work, send, x_grad, gain_grad = call(
        heads_sum,
        (
            struct((FX, ROWS), BF16),
            struct((FX, PASS), BF16),
            struct((FX, ROWS), BF16),
            struct((FX,), F32),
        ),
    )(heads, xt, cot_work, gain)
    got = lax.ppermute(send, DP, down)
    y_owned = call(route_out, struct((FX, SLOTS), BF16))(counts, y_work, got)
    return (y_owned.T, x_grad.T, qkv_grad.T, out_grad, gain_grad)


def solution(mesh):
    fine = Mesh(mesh.devices.reshape(4, 4, 4, 2, 4), DP + ("x",))
    return jax.shard_map(
        shards,
        mesh=fine,
        in_specs=(P(DP, "x"), P("x"), P(None, "x"), P("x", None), P(DP, "x"), P()),
        out_specs=(P(DP, "x"), P(DP, "x"), P(None, "x"), P("x", None), P("x")),
        check_vma=False,
    )
```

```python
import jax
import jax.numpy as jnp
from jax import lax
from jax.experimental import pallas as pl
from jax.experimental.pallas import tpu as pltpu
from jax.sharding import Mesh, PartitionSpec as P

HD = 80
WIN = 64
W_DEV = 6
epsilon = 1e-06

F32 = jnp.float32
BF16 = jnp.bfloat16
DP = ("zh", "zl", "y", "c")

FEAT = 1280
ROWS = 384
FX = 320
QKV = 480
ATT = 160
HEADS = 2
SLOTS = 704
PASS = 320
GROWS = 336

HALF = 25600
Y_LANES = 6400
Z_LANES = 1664
TILE = 128

VMEM = pl.BlockSpec(memory_space=pltpu.VMEM)
ANY = pl.BlockSpec(memory_space=pl.ANY)
HBM = pl.BlockSpec(memory_space=pltpu.HBM)


def call(kernel, out_shapes, ins=None, outs=None, aliases=None, scratch=(), vmem_mib=24, flops=1000000):
    specs = {}
    if ins is not None:
        specs["in_specs"] = ins
    if outs is not None:
        specs["out_specs"] = outs
    return pl.pallas_call(
        kernel,
        out_shape=out_shapes,
        scratch_shapes=list(scratch),
        input_output_aliases=aliases or {},
        compiler_params=pltpu.CompilerParams(vmem_limit_bytes=vmem_mib * 1024 * 1024),
        cost_estimate=pl.CostEstimate(flops=flops, bytes_accessed=1000000, transcendentals=0),
        **specs,
    )


def struct(shape, dtype):
    return jax.ShapeDtypeStruct(shape, dtype)


def drift_of(counts_row, rank):
    owners = lax.broadcasted_iota(jnp.int32, counts_row.shape, 1)
    before = jnp.sum(jnp.where(owners < rank, counts_row, 0), axis=1, keepdims=True)
    return before - rank * W_DEV


def one_hot(rows, cols, shift):
    r = lax.broadcasted_iota(jnp.int32, (rows, cols), 0)
    c = lax.broadcasted_iota(jnp.int32, (rows, cols), 1)
    return jnp.where(r == c + shift, 1.0, 0.0).astype(BF16)


def dot(a, b, dims):
    return lax.dot_general(a, b, ((dims[:1], dims[1:]), ((), ())), preferred_element_type=F32)


def enter(counts_hbm, cot_hbm, send_ref, counts, cot, sems):
    copies = [
        pltpu.make_async_copy(counts_hbm, counts, sems.at[0]),
        pltpu.make_async_copy(cot_hbm, cot, sems.at[1]),
    ]
    for copy in copies:
        copy.start()
    for copy in copies:
        copy.wait()
    drift = drift_of(counts[...], lax.axis_index(DP))
    pick = one_hot(SLOTS, PASS, (W_DEV - drift) * WIN)
    send_ref[...] = dot(cot[...], pick, (1, 0)).astype(BF16)


def route_in(counts_ref, gain_ref, cot_ref, got_ref, out_ref):
    drift = drift_of(counts_ref[...], lax.axis_index(DP)) * WIN
    own = dot(cot_ref[:, :ROWS], one_hot(ROWS, ROWS, -drift), (1, 0))
    col = lax.broadcasted_iota(jnp.int32, (PASS, ROWS), 1)
    row = lax.broadcasted_iota(jnp.int32, (PASS, ROWS), 0)
    near = jnp.where((row == col) & (col < drift), 1.0, 0.0).astype(BF16)
    out_ref[:FX, :] = (own + dot(got_ref[...], near, (1, 0))).astype(BF16)
    out_ref[FX:, :] = jnp.zeros((GROWS - FX, ROWS), BF16)
    out_ref[FX:, :FX] = jnp.broadcast_to(gain_ref[...], (GROWS - FX, FX))


def x_rows(x_ref, i):
    return x_ref[80 * i:80 * (i + 1), :]


def pairs():
    return [(3 * h + p, h, slice(128 * p, 128 * (p + 1)), 3 * HD * h) for h in range(HEADS) for p in range(3)]


def block(x_ref, g_ref, wq_ref, wo_ref, send_ref, keep_ref, gp_ref, mx_ref, gcol_ref, rms_ref, gt, nrm, pk, gm, dsum):
    core = lax.axis_index("c")
    r_i = lax.broadcasted_iota(jnp.int32, (FX, ROWS), 0)
    c_i = lax.broadcasted_iota(jnp.int32, (FX, ROWS), 1)
    total = jnp.zeros((8, ROWS), F32)
    for i in range(16):
        x = x_rows(x_ref, i).astype(F32)
        total += jnp.sum((x * x).reshape(10, 8, ROWS), axis=0)
    rms = lax.rsqrt(jnp.sum(total, axis=0, keepdims=True) / FEAT + epsilon)
    rms_ref[...] = rms
    for j in range(4):
        gt[FX * j:FX * (j + 1), :] = g_ref[j, :FX, :]
        row = g_ref[j, FX:, :].astype(F32)[:1, :]
        gcol_ref[FX * j:FX * (j + 1), :] = jnp.sum(jnp.where(r_i == c_i, row, 0.0), axis=1, keepdims=True)
    for i in range(16):
        s = slice(80 * i, 80 * (i + 1))
        nrm[s, :] = ((x_rows(x_ref, i).astype(F32) * rms) * gcol_ref[s, :]).astype(BF16)
    pk[...] = dot(wq_ref[...], nrm[...], (1, 0)).astype(BF16)
    gm[...] = dot(wo_ref[...], gt[...], (1, 0)).astype(BF16)
    qi = lax.broadcasted_iota(jnp.int32, (128, 128), 0)
    ki = lax.broadcasted_iota(jnp.int32, (128, 128), 1)
    same = (qi < WIN) == (ki < WIN)
    scores = [
        jnp.where(same, dot(pk[b:b + HD, c], pk[b + HD:b + 2 * HD, c], (0, 0)) * HD ** (-0.5), -jnp.inf)
        for _, _, c, b in pairs()
    ]
    dws = [dot(gm[HD * h:HD * (h + 1), c], pk[b + 2 * HD:b + 3 * HD, c], (0, 0)) for _, h, c, b in pairs()]
    exps = [jnp.exp(s - jnp.max(s, axis=1, keepdims=True)) for s in scores]
    probs = [e / jnp.sum(e, axis=1, keepdims=True) for e in exps]
    weights = [p.astype(BF16) for p in probs]
    dss = [
        (p * (dw - jnp.sum(dw * p, axis=1, keepdims=True)) * HD ** (-0.5)).astype(BF16)
        for p, dw in zip(probs, dws)
    ]
    for n, h, c, b in pairs():
        mx_ref[HD * h:HD * (h + 1), c] = dot(pk[b + 2 * HD:b + 3 * HD, c], weights[n], (1, 1)).astype(BF16)
        gp_ref[b:b + HD, c] = dot(pk[b + HD:b + 2 * HD, c], dss[n], (1, 1)).astype(BF16)
        gp_ref[b + HD:b + 2 * HD, c] = dot(pk[b:b + HD, c], dss[n], (1, 0)).astype(BF16)
        gp_ref[b + 2 * HD:b + 3 * HD, c] = dot(gm[HD * h:HD * (h + 1), c], weights[n], (1, 0)).astype(BF16)
    dsum[:QKV, :] = dot(gp_ref[...], nrm[...], (1, 1))
    dsum[QKV:, :] = dot(mx_ref[...], gt[...], (1, 1))
    for i in range(20):
        c = slice(FEAT * i, FEAT * (i + 1))
        keep_ref[:, c] = dsum[pl.ds(pl.multiple_of(core * 320 + 16 * i, 16), 16), :]
        send_ref[:, c] = dsum[pl.ds(pl.multiple_of((1 - core) * 320 + 16 * i, 16), 16), :].astype(BF16)
    total = jnp.zeros((8, FEAT), F32)
    for i in range(30):
        s = slice(16 * i, 16 * (i + 1))
        total += jnp.sum((wq_ref[s, :].astype(F32) * dsum[s, :]).reshape(2, 8, FEAT), axis=0)
    line = jnp.sum(total, axis=0, keepdims=True)
    tile_row = lax.broadcasted_iota(jnp.int32, (16, TILE), 0)
    tile = jnp.zeros((16, TILE), F32)
    for i in range(10):
        tile = jnp.where(tile_row == i, line[:, TILE * i:TILE * (i + 1)], tile)
    tile = tile.astype(BF16)
    send_ref[:, HALF:] = tile
    keep_ref[:, HALF:] = tile.astype(F32)


def head_shares(gp_ref, mx_ref, x_ref, wq_ref, wo_ref, gcol_ref, rms_ref, heads_ref, part, out, sems):
    rms = rms_ref[...]
    part[...] = dot(wo_ref[...], mx_ref[...], (0, 0))
    for j in range(4):
        out[j, :FX, :] = part[FX * j:FX * (j + 1), :].astype(BF16)
    part[...] = dot(wq_ref[...], gp_ref[...], (0, 0))
    row_dot = jnp.zeros((8, ROWS), F32)
    for i in range(16):
        s = slice(80 * i, 80 * (i + 1))
        x = x_rows(x_ref, i).astype(F32)
        row_dot += jnp.sum(((part[s, :] * gcol_ref[s, :]) * (x * rms)).reshape(10, 8, ROWS), axis=0)
    mean = jnp.sum(row_dot, axis=0, keepdims=True) / FEAT
    copies = []
    for j in range(4):
        for i in range(4):
            s = slice(FX * j + 80 * i, FX * j + 80 * (i + 1))
            x = x_rows(x_ref, 4 * j + i).astype(F32)
            z = rms * (part[s, :] * gcol_ref[s, :] - (x * rms) * mean)
            out[j, FX + 80 * i:FX + 80 * (i + 1), :] = z.astype(BF16)
        copies.append(pltpu.make_async_copy(out.at[j], heads_ref.at[j, pl.ds(0, 2 * FX)], sems.at[j]))
        copies[j].start()
    for copy in copies:
        copy.wait()


def core_sum(keep_ref, got_ref, out_ref):
    gain = (keep_ref[:, HALF:] + got_ref[:, HALF:].astype(F32)).astype(BF16)
    for b in range(4):
        s = slice(Y_LANES * b, Y_LANES * (b + 1))
        out_ref[b, :, :Y_LANES] = (keep_ref[:, s] + got_ref[:, s].astype(F32)).astype(BF16)
        out_ref[b, :, Y_LANES:] = gain


def sum_of_four(ref, s):
    a, b, c, d = (ref[i, :, s].astype(F32) for i in range(4))
    return (a + b) + (c + d)


def y_sum(got_ref, out_ref):
    gain = sum_of_four(got_ref, slice(Y_LANES, Y_LANES + TILE)).astype(BF16)
    for b in range(4):
        lo, hi = Z_LANES * b, min(Z_LANES * (b + 1), Y_LANES)
        out_ref[b, :, :hi - lo] = sum_of_four(got_ref, slice(lo, hi)).astype(BF16)
        if hi - lo < Z_LANES:
            out_ref[b, :, hi - lo:Z_LANES] = jnp.zeros((16, Z_LANES - (hi - lo)), BF16)
        out_ref[b, :, Z_LANES:] = gain


def zl_sum(got_ref, out_ref):
    out_ref[...] = sum_of_four(got_ref, slice(None)).astype(BF16)


def pair_sum(own_ref, got_ref, heads_ref, out_ref):
    out_ref[...] = (own_ref[...].astype(F32) + got_ref[...].astype(F32)).astype(BF16)


def zh_sum(own_ref, got_ref, out_ref, tile_ref):
    total = own_ref[...].astype(F32) + got_ref[...].astype(F32)
    out_ref[...] = total[:, :Z_LANES].astype(BF16)
    tile_ref[...] = total[:, Z_LANES:]


def gain_lines(tile_ref, heads_in, heads_ref, lines, sems):
    tile = tile_ref[...]
    line = jnp.concatenate([tile[i:i + 1, :] for i in range(10)], axis=1)
    row = lax.broadcasted_iota(jnp.int32, (16, FX), 0)
    copies = []
    for j in range(4):
        chunk = line[:, FX * j:FX * (j + 1)]
        high = chunk.astype(BF16).astype(F32)
        lines[j] = jnp.zeros((16, ROWS), BF16)
        lines[j, :, :FX] = jnp.where(row == 0, high, jnp.where(row == 1, chunk - high, 0.0)).astype(BF16)
        copies.append(pltpu.make_async_copy(lines.at[j], heads_ref.at[j, pl.ds(2 * FX, 16)], sems.at[j]))
        copies[j].start()
    for copy in copies:
        copy.wait()


def z_pair(own_ref, got_ref, out_ref):
    first = lax.axis_index("zl") < 2

    @pl.when(first)
    def _():
        out_ref[0] = own_ref[...]
        out_ref[1] = got_ref[...]

    @pl.when(jnp.logical_not(first))
    def _():
        out_ref[0] = got_ref[...]
        out_ref[1] = own_ref[...]


def z_pack(own_ref, got_ref, out_ref):
    zl = lax.axis_index("zl")
    outer = (zl == 0) | (zl == 3)

    def place(outer_ref, inner_ref):
        for n, shard in enumerate((outer_ref.at[0], inner_ref.at[0], inner_ref.at[1], outer_ref.at[1])):
            lo, hi = Z_LANES * n, min(Z_LANES * (n + 1), Y_LANES)
            out_ref[:, lo:hi] = shard[:, :hi - lo]

    @pl.when(outer)
    def _():
        place(own_ref, got_ref)

    @pl.when(jnp.logical_not(outer))
    def _():
        place(got_ref, own_ref)


def weights_out(own_ref, other_any, qkv_ref, out_ref, other, buf, sems):
    core = lax.axis_index("c")
    loads = [pltpu.make_async_copy(other_any.at[b], other.at[b], sems.at[8 + b]) for b in range(4)]
    for load in loads:
        load.start()
    for n in range(8):
        b = n % 4
        if n >= 4:
            loads[b].wait()
        ref, half = (own_ref, core) if n < 4 else (other, 1 - core)
        for o in range(5):
            row = 80 * n + 16 * o
            buf[row:row + 16, :] = ref[b, :, FEAT * o:FEAT * (o + 1)].astype(F32)
        chunk = buf.at[pl.ds(80 * n, 80)]

        @pl.when(half == 0)
        def _():
            pltpu.make_async_copy(chunk, qkv_ref.at[pl.ds(80 * b, 80)], sems.at[n]).start()

        @pl.when(half == 1)
        def _():
            target = qkv_ref.at[pl.ds(320 + 80 * b, 80)] if b < 2 else out_ref.at[pl.ds(80 * (b - 2), 80)]
            pltpu.make_async_copy(chunk, target, sems.at[n]).start()

    for n in range(8):
        pltpu.make_async_copy(buf.at[pl.ds(80 * n, 80)], qkv_ref.at[pl.ds(0, 80)], sems.at[n]).wait()


def heads_sum(got_ref, x_ref, cot_ref, gain_ref, y_ref, send_ref, grad_ref, gain_grad_ref):
    for i in range(5):
        s = slice(64 * i, 64 * (i + 1))
        t = slice(FX + 64 * i, FX + 64 * (i + 1))
        a, b, c, d = (got_ref[j, s, :].astype(F32) for j in range(4))
        y = (x_ref[s, :].astype(F32) + ((a + b) + (c + d))).astype(BF16)
        y_ref[s, :] = y
        send_ref[s, :] = y[:, :PASS]
        a, b, c, d = (got_ref[j, t, :].astype(F32) for j in range(4))
        grad_ref[s, :] = (cot_ref[s, :].astype(F32) + ((a + b) + (c + d))).astype(BF16)
    a, b, c, d = (got_ref[j, 2 * FX:, :].astype(F32) for j in range(4))
    line = jnp.sum((a + b) + (c + d), axis=0, keepdims=True)
    gain_grad_ref[...] = (line[:, :FX] / gain_ref[...].astype(F32)).reshape(FX)


def route_out(counts_ref, y_ref, got_ref, out_ref):
    rank = lax.axis_index(DP)
    counts = counts_ref[...]
    owners = lax.broadcasted_iota(jnp.int32, counts.shape, 1)
    live = jnp.sum(jnp.where(owners == rank, counts, 0), axis=1, keepdims=True) * WIN
    drift = drift_of(counts, rank) * WIN
    kept = W_DEV * WIN - drift
    r = lax.broadcasted_iota(jnp.int32, (ROWS, SLOTS), 0)
    c = lax.broadcasted_iota(jnp.int32, (ROWS, SLOTS), 1)
    own = jnp.where((r == c + drift) & (c < live), 1.0, 0.0).astype(BF16)
    r, c = r[:PASS], c[:PASS]
    far = jnp.where((r == c - kept) & (c < live), 1.0, 0.0).astype(BF16)
    out_ref[...] = (dot(y_ref[...], own, (1, 0)) + dot(got_ref[...], far, (1, 0))).astype(BF16)


def shards(x_work, norm_gain, w_qkv, w_out, cot_owned, counts):
    xt, cot, wq = x_work.T, cot_owned.T, w_qkv.T
    counts = counts.reshape(1, -1)
    gain = norm_gain.reshape(1, -1)
    up = [(i, i + 1) for i in range(127)]
    down = [(i + 1, i) for i in range(127)]
    cores = [(0, 1), (1, 0)]

    send = call(
        enter,
        struct((FX, PASS), BF16),
        ins=(HBM, HBM),
        scratch=(pltpu.VMEM((1, 128), jnp.int32), pltpu.VMEM((FX, SLOTS), BF16), pltpu.SemaphoreType.DMA((2,))),
    )(counts, cot)
    got = lax.ppermute(send, DP, up)
    x_full = lax.all_gather(xt, "x", axis=0, tiled=True)
    cot_work = call(route_in, struct((GROWS, ROWS), BF16))(counts, gain, cot, got)
    g_full = lax.all_gather(cot_work, "x", axis=0)

    send, keep, gp, mx, gcol, rms = call(
        block,
        (
            struct((16, HALF + TILE), BF16),
            struct((16, HALF + TILE), F32),
            struct((QKV, ROWS), BF16),
            struct((ATT, ROWS), BF16),
            struct((FEAT, 1), F32),
            struct((1, ROWS), F32),
        ),
        scratch=(
            pltpu.VMEM((FEAT, ROWS), BF16),
            pltpu.VMEM((FEAT, ROWS), BF16),
            pltpu.VMEM((QKV, ROWS), BF16),
            pltpu.VMEM((ATT, ROWS), BF16),
            pltpu.VMEM((QKV + ATT, FEAT), F32),
        ),
        vmem_mib=40,
        flops=1500000000,
    )(x_full, g_full, wq, w_out)

    got = lax.ppermute(send, "c", cores)
    heads_shape = struct((4, 2 * FX + 16, ROWS), BF16)
    heads = call(
        head_shares,
        heads_shape,
        outs=HBM,
        scratch=(
            pltpu.VMEM((FEAT, ROWS), F32),
            pltpu.VMEM((4, 2 * FX, ROWS), BF16),
            pltpu.SemaphoreType.DMA((4,)),
        ),
        vmem_mib=40,
        flops=700000000,
    )(gp, mx, x_full, wq, w_out, gcol, rms)

    parts = call(core_sum, struct((4, 16, Y_LANES + TILE), BF16))(keep, got)
    parts = lax.all_to_all(parts, "y", 0, 0)
    parts = call(y_sum, struct((4, 16, Z_LANES + TILE), BF16))(parts)
    parts = lax.all_to_all(parts, "zl", 0, 0)
    part = call(zl_sum, struct((16, Z_LANES + TILE), BF16))(parts)
    got = lax.ppermute(part, "zh", [(0, 1), (1, 0), (2, 3), (3, 2)])
    part = call(pair_sum, struct((16, Z_LANES + TILE), BF16), ins=(VMEM, VMEM, HBM))(part, got, heads)
    got = lax.ppermute(part, "zh", [(1, 2), (2, 1), (3, 0), (0, 3)])
    part, tile = call(zh_sum, (struct((16, Z_LANES), BF16), struct((16, TILE), F32)))(part, got)
    got = lax.ppermute(part, "zl", [(0, 3), (3, 0), (1, 2), (2, 1)])
    heads = call(
        gain_lines,
        heads_shape,
        ins=(VMEM, HBM),
        outs=HBM,
        aliases={1: 0},
        scratch=(pltpu.VMEM((4, 16, ROWS), BF16), pltpu.SemaphoreType.DMA((4,))),
    )(tile, heads)
    heads = lax.all_to_all(heads, "x", 0, 0)
    pair = call(z_pair, struct((2, 16, Z_LANES), BF16), flops=30000000000)(part, got)
    got = lax.ppermute(pair, "zl", [(0, 1), (1, 0), (2, 3), (3, 2)])
    part = call(z_pack, struct((16, Y_LANES), BF16))(pair, got)
    own = lax.all_gather(part, "y", axis=0)
    other = lax.ppermute(own, "c", cores)
    qkv_grad, out_grad = call(
        weights_out,
        (struct((QKV, FEAT), F32), struct((ATT, FEAT), F32)),
        ins=(VMEM, ANY),
        outs=(ANY, ANY),
        scratch=(
            pltpu.VMEM((4, 16, Y_LANES), BF16),
            pltpu.VMEM((QKV + ATT, FEAT), F32),
            pltpu.SemaphoreType.DMA((12,)),
        ),
    )(own, other)

    y_work, send, x_grad, gain_grad = call(
        heads_sum,
        (
            struct((FX, ROWS), BF16),
            struct((FX, PASS), BF16),
            struct((FX, ROWS), BF16),
            struct((FX,), F32),
        ),
    )(heads, xt, cot_work, gain)
    got = lax.ppermute(send, DP, down)
    y_owned = call(route_out, struct((FX, SLOTS), BF16))(counts, y_work, got)
    return (y_owned.T, x_grad.T, qkv_grad.T, out_grad, gain_grad)


def solution(mesh):
    fine = Mesh(mesh.devices.reshape(4, 4, 4, 2, 4), DP + ("x",))
    return jax.shard_map(
        shards,
        mesh=fine,
        in_specs=(P(DP, "x"), P("x"), P(None, "x"), P("x", None), P(DP, "x"), P()),
        out_specs=(P(DP, "x"), P(DP, "x"), P(None, "x"), P("x", None), P("x")),
        check_vma=False,
    )
```

```python
import jax
import jax.numpy as jnp
from jax import lax
from jax.experimental import pallas as pl
from jax.experimental.pallas import tpu as pltpu
from jax.sharding import Mesh, PartitionSpec as P

HD = 80
WIN = 64
W_DEV = 6
epsilon = 1e-06

F32 = jnp.float32
BF16 = jnp.bfloat16
DP = ("zh", "zl", "y", "c")

FEAT = 1280
ROWS = 384
FX = 320
QKV = 480
ATT = 160
HEADS = 2
SLOTS = 704
PASS = 320
GROWS = 336

HALF = 25600
Y_LANES = 6400
Z_LANES = 1664
TILE = 128

VMEM = pl.BlockSpec(memory_space=pltpu.VMEM)
ANY = pl.BlockSpec(memory_space=pl.ANY)
HBM = pl.BlockSpec(memory_space=pltpu.HBM)


def call(kernel, out_shapes, ins=None, outs=None, aliases=None, scratch=(), vmem_mib=24, flops=1000000):
    specs = {}
    if ins is not None:
        specs["in_specs"] = ins
    if outs is not None:
        specs["out_specs"] = outs
    return pl.pallas_call(
        kernel,
        out_shape=out_shapes,
        scratch_shapes=list(scratch),
        input_output_aliases=aliases or {},
        compiler_params=pltpu.CompilerParams(vmem_limit_bytes=vmem_mib * 1024 * 1024),
        cost_estimate=pl.CostEstimate(flops=flops, bytes_accessed=1000000, transcendentals=0),
        **specs,
    )


def struct(shape, dtype):
    return jax.ShapeDtypeStruct(shape, dtype)


def drift_of(counts_row, rank):
    owners = lax.broadcasted_iota(jnp.int32, counts_row.shape, 1)
    before = jnp.sum(jnp.where(owners < rank, counts_row, 0), axis=1, keepdims=True)
    return before - rank * W_DEV


def one_hot(rows, cols, shift):
    r = lax.broadcasted_iota(jnp.int32, (rows, cols), 0)
    c = lax.broadcasted_iota(jnp.int32, (rows, cols), 1)
    return jnp.where(r == c + shift, 1.0, 0.0).astype(BF16)


def dot(a, b, dims):
    return lax.dot_general(a, b, ((dims[:1], dims[1:]), ((), ())), preferred_element_type=F32)


def route_in(counts_hbm, gain_hbm, cot_hbm, got_hbm, out_ref, counts_ref, gain_ref, cot_ref, got_ref, sems):
    pairs_in = ((counts_hbm, counts_ref), (gain_hbm, gain_ref), (cot_hbm.at[:, pl.ds(0, ROWS)], cot_ref), (got_hbm, got_ref))
    copies = [pltpu.make_async_copy(a, b, sems.at[n]) for n, (a, b) in enumerate(pairs_in)]
    for copy in copies:
        copy.start()
    for copy in copies:
        copy.wait()
    rank = lax.axis_index(DP)
    drift = drift_of(counts_ref[...], rank) * WIN
    drift_before = drift_of(counts_ref[...], rank - 1) * WIN
    own = dot(cot_ref[...], one_hot(ROWS, ROWS, -drift), (1, 0))
    col = lax.broadcasted_iota(jnp.int32, (SLOTS, ROWS), 1)
    row = lax.broadcasted_iota(jnp.int32, (SLOTS, ROWS), 0)
    near = jnp.where((row == col + (W_DEV * WIN - drift_before)) & (col < drift), 1.0, 0.0).astype(BF16)
    out_ref[:FX, :] = (own + dot(got_ref[...], near, (1, 0))).astype(BF16)
    out_ref[FX:, :] = jnp.zeros((GROWS - FX, ROWS), BF16)
    out_ref[FX:, :FX] = jnp.broadcast_to(gain_ref[...].reshape(1, FX), (GROWS - FX, FX))


def x_rows(x_ref, i):
    return x_ref[80 * i:80 * (i + 1), :]


def pairs():
    return [(3 * h + p, h, slice(128 * p, 128 * (p + 1)), 3 * HD * h) for h in range(HEADS) for p in range(3)]


def block(x_ref, g_ref, wq_ref, wo_ref, send_ref, dsum, tile_ref, gp_ref, mx_ref, gcol_ref, rms_ref, gt, nrm, pk, gm):
    core = lax.axis_index("c")
    r_i = lax.broadcasted_iota(jnp.int32, (FX, ROWS), 0)
    c_i = lax.broadcasted_iota(jnp.int32, (FX, ROWS), 1)
    total = jnp.zeros((8, ROWS), F32)
    for i in range(16):
        x = x_rows(x_ref, i).astype(F32)
        total += jnp.sum((x * x).reshape(10, 8, ROWS), axis=0)
    rms = lax.rsqrt(jnp.sum(total, axis=0, keepdims=True) / FEAT + epsilon)
    rms_ref[...] = rms
    for j in range(4):
        gt[FX * j:FX * (j + 1), :] = g_ref[j, :FX, :]
        row = g_ref[j, FX:, :].astype(F32)[:1, :]
        gcol_ref[FX * j:FX * (j + 1), :] = jnp.sum(jnp.where(r_i == c_i, row, 0.0), axis=1, keepdims=True)
    for i in range(16):
        s = slice(80 * i, 80 * (i + 1))
        nrm[s, :] = ((x_rows(x_ref, i).astype(F32) * rms) * gcol_ref[s, :]).astype(BF16)
    pk[...] = dot(wq_ref[...], nrm[...], (1, 0)).astype(BF16)
    gm[...] = dot(wo_ref[...], gt[...], (1, 0)).astype(BF16)
    qi = lax.broadcasted_iota(jnp.int32, (128, 128), 0)
    ki = lax.broadcasted_iota(jnp.int32, (128, 128), 1)
    same = (qi < WIN) == (ki < WIN)
    scores = [
        jnp.where(same, dot(pk[b:b + HD, c], pk[b + HD:b + 2 * HD, c], (0, 0)) * HD ** (-0.5), -jnp.inf)
        for _, _, c, b in pairs()
    ]
    dws = [dot(gm[HD * h:HD * (h + 1), c], pk[b + 2 * HD:b + 3 * HD, c], (0, 0)) for _, h, c, b in pairs()]
    exps = [jnp.exp(s - jnp.max(s, axis=1, keepdims=True)) for s in scores]
    probs = [e / jnp.sum(e, axis=1, keepdims=True) for e in exps]
    weights = [p.astype(BF16) for p in probs]
    dss = [
        (p * (dw - jnp.sum(dw * p, axis=1, keepdims=True)) * HD ** (-0.5)).astype(BF16)
        for p, dw in zip(probs, dws)
    ]
    for n, h, c, b in pairs():
        mx_ref[HD * h:HD * (h + 1), c] = dot(pk[b + 2 * HD:b + 3 * HD, c], weights[n], (1, 1)).astype(BF16)
        gp_ref[b:b + HD, c] = dot(pk[b + HD:b + 2 * HD, c], dss[n], (1, 1)).astype(BF16)
        gp_ref[b + HD:b + 2 * HD, c] = dot(pk[b:b + HD, c], dss[n], (1, 0)).astype(BF16)
        gp_ref[b + 2 * HD:b + 3 * HD, c] = dot(gm[HD * h:HD * (h + 1), c], weights[n], (1, 0)).astype(BF16)
    dsum[:QKV, :] = dot(gp_ref[...], nrm[...], (1, 1))
    dsum[QKV:, :] = dot(mx_ref[...], gt[...], (1, 1))
    for i in range(20):
        c = slice(FEAT * i, FEAT * (i + 1))
        send_ref[:, c] = dsum[pl.ds(pl.multiple_of((1 - core) * 320 + 16 * i, 16), 16), :].astype(BF16)
    total = jnp.zeros((8, FEAT), F32)
    for i in range(30):
        s = slice(16 * i, 16 * (i + 1))
        total += jnp.sum((wq_ref[s, :].astype(F32) * dsum[s, :]).reshape(2, 8, FEAT), axis=0)
    line = jnp.sum(total, axis=0, keepdims=True)
    tile_row = lax.broadcasted_iota(jnp.int32, (16, TILE), 0)
    tile = jnp.zeros((16, TILE), F32)
    for i in range(10):
        tile = jnp.where(tile_row == i, line[:, TILE * i:TILE * (i + 1)], tile)
    tile = tile.astype(BF16)
    send_ref[:, HALF:] = tile
    tile_ref[...] = tile.astype(F32)


def head_shares(gp_ref, mx_ref, x_ref, wq_ref, wo_ref, gcol_ref, rms_ref, heads_ref, part, out, sems):
    rms = rms_ref[...]
    part[...] = dot(wo_ref[...], mx_ref[...], (0, 0))
    for j in range(4):
        out[j, :FX, :] = part[FX * j:FX * (j + 1), :].astype(BF16)
    part[...] = dot(wq_ref[...], gp_ref[...], (0, 0))
    row_dot = jnp.zeros((8, ROWS), F32)
    for i in range(16):
        s = slice(80 * i, 80 * (i + 1))
        x = x_rows(x_ref, i).astype(F32)
        row_dot += jnp.sum(((part[s, :] * gcol_ref[s, :]) * (x * rms)).reshape(10, 8, ROWS), axis=0)
    mean = jnp.sum(row_dot, axis=0, keepdims=True) / FEAT
    copies = []
    for j in range(4):
        for i in range(4):
            s = slice(FX * j + 80 * i, FX * j + 80 * (i + 1))
            x = x_rows(x_ref, 4 * j + i).astype(F32)
            z = rms * (part[s, :] * gcol_ref[s, :] - (x * rms) * mean)
            out[j, FX + 80 * i:FX + 80 * (i + 1), :] = z.astype(BF16)
        copies.append(pltpu.make_async_copy(out.at[j], heads_ref.at[j, pl.ds(0, 2 * FX)], sems.at[j]))
        copies[j].start()
    for copy in copies:
        copy.wait()


def core_sum(dsum_ref, tile_ref, got_ref, out_ref):
    core = lax.axis_index("c")
    gain = (tile_ref[...] + got_ref[:, HALF:].astype(F32)).astype(BF16)
    for i in range(20):
        b, o = divmod(i, 5)
        own = dsum_ref[pl.ds(pl.multiple_of(core * 320 + 16 * i, 16), 16), :]
        got = got_ref[:, FEAT * i:FEAT * (i + 1)].astype(F32)
        out_ref[b, :, FEAT * o:FEAT * (o + 1)] = (own + got).astype(BF16)
    for b in range(4):
        out_ref[b, :, Y_LANES:] = gain


def sum_of_four(ref, s):
    a, b, c, d = (ref[i, :, s].astype(F32) for i in range(4))
    return (a + b) + (c + d)


def y_sum(got_ref, out_ref):
    gain = sum_of_four(got_ref, slice(Y_LANES, Y_LANES + TILE)).astype(BF16)
    for b in range(4):
        lo, hi = Z_LANES * b, min(Z_LANES * (b + 1), Y_LANES)
        out_ref[b, :, :hi - lo] = sum_of_four(got_ref, slice(lo, hi)).astype(BF16)
        if hi - lo < Z_LANES:
            out_ref[b, :, hi - lo:Z_LANES] = jnp.zeros((16, Z_LANES - (hi - lo)), BF16)
        out_ref[b, :, Z_LANES:] = gain


def zl_sum(got_ref, out_ref):
    out_ref[...] = sum_of_four(got_ref, slice(None)).astype(BF16)


def pair_sum(own_ref, got_ref, heads_ref, out_ref):
    out_ref[...] = (own_ref[...].astype(F32) + got_ref[...].astype(F32)).astype(BF16)


def zh_sum(own_ref, got_ref, out_ref, tile_ref):
    total = own_ref[...].astype(F32) + got_ref[...].astype(F32)
    out_ref[...] = total[:, :Z_LANES].astype(BF16)
    tile_ref[...] = total[:, Z_LANES:]


def gain_lines(tile_ref, heads_in, heads_ref, lines, sems):
    tile = tile_ref[...]
    line = jnp.concatenate([tile[i:i + 1, :] for i in range(10)], axis=1)
    row = lax.broadcasted_iota(jnp.int32, (16, FX), 0)
    copies = []
    for j in range(4):
        chunk = line[:, FX * j:FX * (j + 1)]
        high = chunk.astype(BF16).astype(F32)
        lines[j] = jnp.zeros((16, ROWS), BF16)
        lines[j, :, :FX] = jnp.where(row == 0, high, jnp.where(row == 1, chunk - high, 0.0)).astype(BF16)
        copies.append(pltpu.make_async_copy(lines.at[j], heads_ref.at[j, pl.ds(2 * FX, 16)], sems.at[j]))
        copies[j].start()
    for copy in copies:
        copy.wait()


def z_pair(own_ref, got_ref, out_ref):
    first = lax.axis_index("zl") < 2

    @pl.when(first)
    def _():
        out_ref[0] = own_ref[...]
        out_ref[1] = got_ref[...]

    @pl.when(jnp.logical_not(first))
    def _():
        out_ref[0] = got_ref[...]
        out_ref[1] = own_ref[...]


def z_pack(own_ref, got_ref, out_ref):
    zl = lax.axis_index("zl")
    outer = (zl == 0) | (zl == 3)

    def place(outer_ref, inner_ref):
        for n, shard in enumerate((outer_ref.at[0], inner_ref.at[0], inner_ref.at[1], outer_ref.at[1])):
            lo, hi = Z_LANES * n, min(Z_LANES * (n + 1), Y_LANES)
            out_ref[:, lo:hi] = shard[:, :hi - lo]

    @pl.when(outer)
    def _():
        place(own_ref, got_ref)

    @pl.when(jnp.logical_not(outer))
    def _():
        place(got_ref, own_ref)


def weights_out(own_ref, other_any, qkv_ref, out_ref, other, buf, sems):
    core = lax.axis_index("c")
    loads = [pltpu.make_async_copy(other_any.at[b], other.at[b], sems.at[8 + b]) for b in range(4)]
    for load in loads:
        load.start()
    for n in range(8):
        b = n % 4
        if n >= 4:
            loads[b].wait()
        ref, half = (own_ref, core) if n < 4 else (other, 1 - core)
        for o in range(5):
            row = 80 * n + 16 * o
            buf[row:row + 16, :] = ref[b, :, FEAT * o:FEAT * (o + 1)].astype(F32)
        chunk = buf.at[pl.ds(80 * n, 80)]

        @pl.when(half == 0)
        def _():
            pltpu.make_async_copy(chunk, qkv_ref.at[pl.ds(80 * b, 80)], sems.at[n]).start()

        @pl.when(half == 1)
        def _():
            target = qkv_ref.at[pl.ds(320 + 80 * b, 80)] if b < 2 else out_ref.at[pl.ds(80 * (b - 2), 80)]
            pltpu.make_async_copy(chunk, target, sems.at[n]).start()

    for n in range(8):
        pltpu.make_async_copy(buf.at[pl.ds(80 * n, 80)], qkv_ref.at[pl.ds(0, 80)], sems.at[n]).wait()


def heads_sum(got_ref, x_ref, cot_ref, gain_ref, y_ref, send_ref, grad_ref, gain_grad_ref):
    for i in range(5):
        s = slice(64 * i, 64 * (i + 1))
        t = slice(FX + 64 * i, FX + 64 * (i + 1))
        a, b, c, d = (got_ref[j, s, :].astype(F32) for j in range(4))
        y = (x_ref[s, :].astype(F32) + ((a + b) + (c + d))).astype(BF16)
        y_ref[s, :] = y
        send_ref[s, :] = y[:, :PASS]
        a, b, c, d = (got_ref[j, t, :].astype(F32) for j in range(4))
        grad_ref[s, :] = (cot_ref[s, :].astype(F32) + ((a + b) + (c + d))).astype(BF16)
    a, b, c, d = (got_ref[j, 2 * FX:, :].astype(F32) for j in range(4))
    line = jnp.sum((a + b) + (c + d), axis=0, keepdims=True)
    gain_grad_ref[...] = (line[:, :FX] / gain_ref[...].astype(F32)).reshape(FX)


def route_out(counts_ref, y_ref, got_ref, out_ref):
    rank = lax.axis_index(DP)
    counts = counts_ref[...]
    owners = lax.broadcasted_iota(jnp.int32, counts.shape, 1)
    live = jnp.sum(jnp.where(owners == rank, counts, 0), axis=1, keepdims=True) * WIN
    drift = drift_of(counts, rank) * WIN
    kept = W_DEV * WIN - drift
    r = lax.broadcasted_iota(jnp.int32, (ROWS, SLOTS), 0)
    c = lax.broadcasted_iota(jnp.int32, (ROWS, SLOTS), 1)
    own = jnp.where((r == c + drift) & (c < live), 1.0, 0.0).astype(BF16)
    r, c = r[:PASS], c[:PASS]
    far = jnp.where((r == c - kept) & (c < live), 1.0, 0.0).astype(BF16)
    out_ref[...] = (dot(y_ref[...], own, (1, 0)) + dot(got_ref[...], far, (1, 0))).astype(BF16)


def shards(x_work, norm_gain, w_qkv, w_out, cot_owned, counts):
    xt, cot, wq = x_work.T, cot_owned.T, w_qkv.T
    counts = counts.reshape(1, -1)
    gain = norm_gain.reshape(1, -1)
    up = [(i, i + 1) for i in range(127)]
    down = [(i + 1, i) for i in range(127)]
    cores = [(0, 1), (1, 0)]

    got = lax.ppermute(cot, DP, up)
    x_full = lax.all_gather(xt, "x", axis=0, tiled=True)
    cot_work = call(
        route_in,
        struct((GROWS, ROWS), BF16),
        ins=(HBM, HBM, HBM, HBM),
        scratch=(
            pltpu.VMEM((1, 128), jnp.int32),
            pltpu.VMEM((FX,), BF16),
            pltpu.VMEM((FX, ROWS), BF16),
            pltpu.VMEM((FX, SLOTS), BF16),
            pltpu.SemaphoreType.DMA((4,)),
        ),
        vmem_mib=61,
    )(counts, norm_gain, cot, got)
    g_full = lax.all_gather(cot_work, "x", axis=0)

    send, dsum, tile, gp, mx, gcol, rms = call(
        block,
        (
            struct((16, HALF + TILE), BF16),
            struct((QKV + ATT, FEAT), F32),
            struct((16, TILE), F32),
            struct((QKV, ROWS), BF16),
            struct((ATT, ROWS), BF16),
            struct((FEAT, 1), F32),
            struct((1, ROWS), F32),
        ),
        scratch=(
            pltpu.VMEM((FEAT, ROWS), BF16),
            pltpu.VMEM((FEAT, ROWS), BF16),
            pltpu.VMEM((QKV, ROWS), BF16),
            pltpu.VMEM((ATT, ROWS), BF16),
        ),
        vmem_mib=40,
        flops=1500000000,
    )(x_full, g_full, wq, w_out)

    got = lax.ppermute(send, "c", cores)
    heads_shape = struct((4, 2 * FX + 16, ROWS), BF16)
    heads = call(
        head_shares,
        heads_shape,
        outs=HBM,
        scratch=(
            pltpu.VMEM((FEAT, ROWS), F32),
            pltpu.VMEM((4, 2 * FX, ROWS), BF16),
            pltpu.SemaphoreType.DMA((4,)),
        ),
        vmem_mib=40,
        flops=700000000,
    )(gp, mx, x_full, wq, w_out, gcol, rms)

    parts = call(core_sum, struct((4, 16, Y_LANES + TILE), BF16))(dsum, tile, got)
    parts = lax.all_to_all(parts, "y", 0, 0)
    parts = call(y_sum, struct((4, 16, Z_LANES + TILE), BF16))(parts)
    parts = lax.all_to_all(parts, "zl", 0, 0)
    part = call(zl_sum, struct((16, Z_LANES + TILE), BF16))(parts)
    got = lax.ppermute(part, "zh", [(0, 1), (1, 0), (2, 3), (3, 2)])
    part = call(pair_sum, struct((16, Z_LANES + TILE), BF16), ins=(VMEM, VMEM, HBM))(part, got, heads)
    got = lax.ppermute(part, "zh", [(1, 2), (2, 1), (3, 0), (0, 3)])
    part, tile = call(zh_sum, (struct((16, Z_LANES), BF16), struct((16, TILE), F32)))(part, got)
    got = lax.ppermute(part, "zl", [(0, 3), (3, 0), (1, 2), (2, 1)])
    heads = call(
        gain_lines,
        heads_shape,
        ins=(VMEM, HBM),
        outs=HBM,
        aliases={1: 0},
        scratch=(pltpu.VMEM((4, 16, ROWS), BF16), pltpu.SemaphoreType.DMA((4,))),
    )(tile, heads)
    heads = lax.all_to_all(heads, "x", 0, 0)
    pair = call(z_pair, struct((2, 16, Z_LANES), BF16), flops=30000000000)(part, got)
    got = lax.ppermute(pair, "zl", [(0, 1), (1, 0), (2, 3), (3, 2)])
    part = call(z_pack, struct((16, Y_LANES), BF16))(pair, got)
    own = lax.all_gather(part, "y", axis=0)
    other = lax.ppermute(own, "c", cores)
    qkv_grad, out_grad = call(
        weights_out,
        (struct((QKV, FEAT), F32), struct((ATT, FEAT), F32)),
        ins=(VMEM, ANY),
        outs=(ANY, ANY),
        scratch=(
            pltpu.VMEM((4, 16, Y_LANES), BF16),
            pltpu.VMEM((QKV + ATT, FEAT), F32),
            pltpu.SemaphoreType.DMA((12,)),
        ),
    )(own, other)

    y_work, send, x_grad, gain_grad = call(
        heads_sum,
        (
            struct((FX, ROWS), BF16),
            struct((FX, PASS), BF16),
            struct((FX, ROWS), BF16),
            struct((FX,), F32),
        ),
    )(heads, xt, cot_work, gain)
    got = lax.ppermute(send, DP, down)
    y_owned = call(route_out, struct((FX, SLOTS), BF16))(counts, y_work, got)
    return (y_owned.T, x_grad.T, qkv_grad.T, out_grad, gain_grad)


def solution(mesh):
    fine = Mesh(mesh.devices.reshape(4, 4, 4, 2, 4), DP + ("x",))
    return jax.shard_map(
        shards,
        mesh=fine,
        in_specs=(P(DP, "x"), P("x"), P(None, "x"), P("x", None), P(DP, "x"), P()),
        out_specs=(P(DP, "x"), P(DP, "x"), P(None, "x"), P("x", None), P("x")),
        check_vma=False,
    )
```

```python
import jax
import jax.numpy as jnp
from jax import lax
from jax.experimental import pallas as pl
from jax.experimental.pallas import tpu as pltpu
from jax.sharding import Mesh, PartitionSpec as P

HD = 80
WIN = 64
W_DEV = 6
epsilon = 1e-06

F32 = jnp.float32
BF16 = jnp.bfloat16
DP = ("zh", "zl", "y", "c")

FEAT = 1280
ROWS = 384
FX = 320
QKV = 480
ATT = 160
HEADS = 2
SLOTS = 704
PASS = 320
GROWS = 336

HALF = 25600
Y_LANES = 6400
Z_LANES = 1664
TILE = 128

VMEM = pl.BlockSpec(memory_space=pltpu.VMEM)
ANY = pl.BlockSpec(memory_space=pl.ANY)
HBM = pl.BlockSpec(memory_space=pltpu.HBM)


def call(kernel, out_shapes, ins=None, outs=None, aliases=None, scratch=(), vmem_mib=24, flops=1000000):
    specs = {}
    if ins is not None:
        specs["in_specs"] = ins
    if outs is not None:
        specs["out_specs"] = outs
    return pl.pallas_call(
        kernel,
        out_shape=out_shapes,
        scratch_shapes=list(scratch),
        input_output_aliases=aliases or {},
        compiler_params=pltpu.CompilerParams(vmem_limit_bytes=vmem_mib * 1024 * 1024),
        cost_estimate=pl.CostEstimate(flops=flops, bytes_accessed=1000000, transcendentals=0),
        **specs,
    )


def struct(shape, dtype):
    return jax.ShapeDtypeStruct(shape, dtype)


def drift_of(counts_row, rank):
    owners = lax.broadcasted_iota(jnp.int32, counts_row.shape, 1)
    before = jnp.sum(jnp.where(owners < rank, counts_row, 0), axis=1, keepdims=True)
    return before - rank * W_DEV


def one_hot(rows, cols, shift):
    r = lax.broadcasted_iota(jnp.int32, (rows, cols), 0)
    c = lax.broadcasted_iota(jnp.int32, (rows, cols), 1)
    return jnp.where(r == c + shift, 1.0, 0.0).astype(BF16)


def dot(a, b, dims):
    return lax.dot_general(a, b, ((dims[:1], dims[1:]), ((), ())), preferred_element_type=F32)


def route_in(counts_hbm, gain_hbm, cot_hbm, got_hbm, out_hbm, counts, gain, cot, got, out, sems):
    loads = ((counts_hbm, counts), (gain_hbm, gain), (cot_hbm.at[:, pl.ds(0, ROWS)], cot), (got_hbm, got))
    loads = [pltpu.make_async_copy(a, b, sems.at[n]) for n, (a, b) in enumerate(loads)]
    for load in loads:
        load.start()
    loads[0].wait()
    rank = lax.axis_index(DP)
    drift = drift_of(counts[...], rank) * WIN
    drift_before = drift_of(counts[...], rank - 1) * WIN
    own = one_hot(ROWS, ROWS, -drift)
    col = lax.broadcasted_iota(jnp.int32, (SLOTS, ROWS), 1)
    row = lax.broadcasted_iota(jnp.int32, (SLOTS, ROWS), 0)
    near = jnp.where((row == col + (W_DEV * WIN - drift_before)) & (col < drift), 1.0, 0.0).astype(BF16)
    loads[1].wait()
    out[FX:, :] = jnp.zeros((GROWS - FX, ROWS), BF16)
    out[FX:, :FX] = jnp.broadcast_to(gain[...].reshape(1, FX), (GROWS - FX, FX))
    loads[2].wait()
    loads[3].wait()
    stores = []
    for n, (lo, hi) in enumerate(((0, 160), (160, FX))):
        block_rows = dot(cot[lo:hi, :], own, (1, 0)) + dot(got[lo:hi, :], near, (1, 0))
        out[lo:hi, :] = block_rows.astype(BF16)
        end = hi if n == 0 else GROWS
        rows = pl.ds(lo, end - lo)
        stores.append(pltpu.make_async_copy(out.at[rows], out_hbm.at[rows], sems.at[4 + n]))
        stores[n].start()
    for store in stores:
        store.wait()


def x_rows(x_ref, i):
    return x_ref[80 * i:80 * (i + 1), :]


def pairs():
    return [(3 * h + p, h, slice(128 * p, 128 * (p + 1)), 3 * HD * h) for h in range(HEADS) for p in range(3)]


def block(x_ref, g_ref, wq_ref, wo_ref, send_ref, dsum, tile_ref, gp_ref, mx_ref, gcol_ref, rms_ref, gt, nrm, pk, gm):
    core = lax.axis_index("c")
    r_i = lax.broadcasted_iota(jnp.int32, (FX, ROWS), 0)
    c_i = lax.broadcasted_iota(jnp.int32, (FX, ROWS), 1)
    total = jnp.zeros((8, ROWS), F32)
    for i in range(16):
        x = x_rows(x_ref, i).astype(F32)
        total += jnp.sum((x * x).reshape(10, 8, ROWS), axis=0)
    rms = lax.rsqrt(jnp.sum(total, axis=0, keepdims=True) / FEAT + epsilon)
    rms_ref[...] = rms
    for j in range(4):
        gt[FX * j:FX * (j + 1), :] = g_ref[j, :FX, :]
        row = g_ref[j, FX:, :].astype(F32)[:1, :]
        gcol_ref[FX * j:FX * (j + 1), :] = jnp.sum(jnp.where(r_i == c_i, row, 0.0), axis=1, keepdims=True)
    for i in range(16):
        s = slice(80 * i, 80 * (i + 1))
        nrm[s, :] = ((x_rows(x_ref, i).astype(F32) * rms) * gcol_ref[s, :]).astype(BF16)
    pk[...] = dot(wq_ref[...], nrm[...], (1, 0)).astype(BF16)
    gm[...] = dot(wo_ref[...], gt[...], (1, 0)).astype(BF16)
    qi = lax.broadcasted_iota(jnp.int32, (128, 128), 0)
    ki = lax.broadcasted_iota(jnp.int32, (128, 128), 1)
    same = (qi < WIN) == (ki < WIN)
    scores = [
        jnp.where(same, dot(pk[b:b + HD, c], pk[b + HD:b + 2 * HD, c], (0, 0)) * HD ** (-0.5), -jnp.inf)
        for _, _, c, b in pairs()
    ]
    dws = [dot(gm[HD * h:HD * (h + 1), c], pk[b + 2 * HD:b + 3 * HD, c], (0, 0)) for _, h, c, b in pairs()]
    exps = [jnp.exp(s - jnp.max(s, axis=1, keepdims=True)) for s in scores]
    probs = [e / jnp.sum(e, axis=1, keepdims=True) for e in exps]
    weights = [p.astype(BF16) for p in probs]
    dss = [
        (p * (dw - jnp.sum(dw * p, axis=1, keepdims=True)) * HD ** (-0.5)).astype(BF16)
        for p, dw in zip(probs, dws)
    ]
    for n, h, c, b in pairs():
        mx_ref[HD * h:HD * (h + 1), c] = dot(pk[b + 2 * HD:b + 3 * HD, c], weights[n], (1, 1)).astype(BF16)
        gp_ref[b:b + HD, c] = dot(pk[b + HD:b + 2 * HD, c], dss[n], (1, 1)).astype(BF16)
        gp_ref[b + HD:b + 2 * HD, c] = dot(pk[b:b + HD, c], dss[n], (1, 0)).astype(BF16)
        gp_ref[b + 2 * HD:b + 3 * HD, c] = dot(gm[HD * h:HD * (h + 1), c], weights[n], (1, 0)).astype(BF16)
    dsum[:QKV, :] = dot(gp_ref[...], nrm[...], (1, 1))
    dsum[QKV:, :] = dot(mx_ref[...], gt[...], (1, 1))
    for i in range(20):
        c = slice(FEAT * i, FEAT * (i + 1))
        send_ref[:, c] = dsum[pl.ds(pl.multiple_of((1 - core) * 320 + 16 * i, 16), 16), :].astype(BF16)
    total = jnp.zeros((8, FEAT), F32)
    for i in range(30):
        s = slice(16 * i, 16 * (i + 1))
        total += jnp.sum((wq_ref[s, :].astype(F32) * dsum[s, :]).reshape(2, 8, FEAT), axis=0)
    line = jnp.sum(total, axis=0, keepdims=True)
    tile_row = lax.broadcasted_iota(jnp.int32, (16, TILE), 0)
    tile = jnp.zeros((16, TILE), F32)
    for i in range(10):
        tile = jnp.where(tile_row == i, line[:, TILE * i:TILE * (i + 1)], tile)
    tile = tile.astype(BF16)
    send_ref[:, HALF:] = tile
    tile_ref[...] = tile.astype(F32)


def head_shares(gp_ref, mx_ref, x_ref, wq_ref, wo_ref, gcol_ref, rms_ref, heads_ref, part, out, sems):
    rms = rms_ref[...]
    part[...] = dot(wo_ref[...], mx_ref[...], (0, 0))
    for j in range(4):
        out[j, :FX, :] = part[FX * j:FX * (j + 1), :].astype(BF16)
    part[...] = dot(wq_ref[...], gp_ref[...], (0, 0))
    row_dot = jnp.zeros((8, ROWS), F32)
    for i in range(16):
        s = slice(80 * i, 80 * (i + 1))
        x = x_rows(x_ref, i).astype(F32)
        row_dot += jnp.sum(((part[s, :] * gcol_ref[s, :]) * (x * rms)).reshape(10, 8, ROWS), axis=0)
    mean = jnp.sum(row_dot, axis=0, keepdims=True) / FEAT
    copies = []
    for j in range(4):
        for i in range(4):
            s = slice(FX * j + 80 * i, FX * j + 80 * (i + 1))
            x = x_rows(x_ref, 4 * j + i).astype(F32)
            z = rms * (part[s, :] * gcol_ref[s, :] - (x * rms) * mean)
            out[j, FX + 80 * i:FX + 80 * (i + 1), :] = z.astype(BF16)
        copies.append(pltpu.make_async_copy(out.at[j], heads_ref.at[j, pl.ds(0, 2 * FX)], sems.at[j]))
        copies[j].start()
    for copy in copies:
        copy.wait()


def core_sum(dsum_ref, tile_ref, got_ref, out_ref):
    core = lax.axis_index("c")
    gain = (tile_ref[...] + got_ref[:, HALF:].astype(F32)).astype(BF16)
    for i in range(20):
        b, o = divmod(i, 5)
        own = dsum_ref[pl.ds(pl.multiple_of(core * 320 + 16 * i, 16), 16), :]
        got = got_ref[:, FEAT * i:FEAT * (i + 1)].astype(F32)
        out_ref[b, :, FEAT * o:FEAT * (o + 1)] = (own + got).astype(BF16)
    for b in range(4):
        out_ref[b, :, Y_LANES:] = gain


def sum_of_four(ref, s):
    a, b, c, d = (ref[i, :, s].astype(F32) for i in range(4))
    return (a + b) + (c + d)


def y_sum(got_ref, out_ref):
    gain = sum_of_four(got_ref, slice(Y_LANES, Y_LANES + TILE)).astype(BF16)
    for b in range(4):
        lo, hi = Z_LANES * b, min(Z_LANES * (b + 1), Y_LANES)
        out_ref[b, :, :hi - lo] = sum_of_four(got_ref, slice(lo, hi)).astype(BF16)
        if hi - lo < Z_LANES:
            out_ref[b, :, hi - lo:Z_LANES] = jnp.zeros((16, Z_LANES - (hi - lo)), BF16)
        out_ref[b, :, Z_LANES:] = gain


def zl_sum(got_ref, out_ref):
    out_ref[...] = sum_of_four(got_ref, slice(None)).astype(BF16)


def pair_sum(own_ref, got_ref, heads_ref, out_ref):
    out_ref[...] = (own_ref[...].astype(F32) + got_ref[...].astype(F32)).astype(BF16)


def zh_sum(own_ref, got_ref, out_ref, tile_ref):
    total = own_ref[...].astype(F32) + got_ref[...].astype(F32)
    out_ref[...] = total[:, :Z_LANES].astype(BF16)
    tile_ref[...] = total[:, Z_LANES:]


def gain_lines(tile_ref, heads_in, heads_ref, lines, sems):
    tile = tile_ref[...]
    line = jnp.concatenate([tile[i:i + 1, :] for i in range(10)], axis=1)
    row = lax.broadcasted_iota(jnp.int32, (16, FX), 0)
    copies = []
    for j in range(4):
        chunk = line[:, FX * j:FX * (j + 1)]
        high = chunk.astype(BF16).astype(F32)
        lines[j] = jnp.zeros((16, ROWS), BF16)
        lines[j, :, :FX] = jnp.where(row == 0, high, jnp.where(row == 1, chunk - high, 0.0)).astype(BF16)
        copies.append(pltpu.make_async_copy(lines.at[j], heads_ref.at[j, pl.ds(2 * FX, 16)], sems.at[j]))
        copies[j].start()
    for copy in copies:
        copy.wait()


def z_pair(own_ref, got_ref, out_ref):
    first = lax.axis_index("zl") < 2

    @pl.when(first)
    def _():
        out_ref[0] = own_ref[...]
        out_ref[1] = got_ref[...]

    @pl.when(jnp.logical_not(first))
    def _():
        out_ref[0] = got_ref[...]
        out_ref[1] = own_ref[...]


def z_pack(own_ref, got_ref, out_ref):
    zl = lax.axis_index("zl")
    outer = (zl == 0) | (zl == 3)

    def place(outer_ref, inner_ref):
        for n, shard in enumerate((outer_ref.at[0], inner_ref.at[0], inner_ref.at[1], outer_ref.at[1])):
            lo, hi = Z_LANES * n, min(Z_LANES * (n + 1), Y_LANES)
            out_ref[:, lo:hi] = shard[:, :hi - lo]

    @pl.when(outer)
    def _():
        place(own_ref, got_ref)

    @pl.when(jnp.logical_not(outer))
    def _():
        place(got_ref, own_ref)


def weights_out(own_ref, other_any, qkv_ref, out_ref, other, buf, sems):
    core = lax.axis_index("c")
    loads = [pltpu.make_async_copy(other_any.at[b], other.at[b], sems.at[8 + b]) for b in range(4)]
    for load in loads:
        load.start()
    for n in range(8):
        b = n % 4
        if n >= 4:
            loads[b].wait()
        ref, half = (own_ref, core) if n < 4 else (other, 1 - core)
        for o in range(5):
            row = 80 * n + 16 * o
            buf[row:row + 16, :] = ref[b, :, FEAT * o:FEAT * (o + 1)].astype(F32)
        chunk = buf.at[pl.ds(80 * n, 80)]

        @pl.when(half == 0)
        def _():
            pltpu.make_async_copy(chunk, qkv_ref.at[pl.ds(80 * b, 80)], sems.at[n]).start()

        @pl.when(half == 1)
        def _():
            target = qkv_ref.at[pl.ds(320 + 80 * b, 80)] if b < 2 else out_ref.at[pl.ds(80 * (b - 2), 80)]
            pltpu.make_async_copy(chunk, target, sems.at[n]).start()

    for n in range(8):
        pltpu.make_async_copy(buf.at[pl.ds(80 * n, 80)], qkv_ref.at[pl.ds(0, 80)], sems.at[n]).wait()


def heads_sum(got_ref, x_ref, cot_ref, gain_ref, y_ref, send_ref, grad_ref, gain_grad_ref):
    for i in range(5):
        s = slice(64 * i, 64 * (i + 1))
        t = slice(FX + 64 * i, FX + 64 * (i + 1))
        a, b, c, d = (got_ref[j, s, :].astype(F32) for j in range(4))
        y = (x_ref[s, :].astype(F32) + ((a + b) + (c + d))).astype(BF16)
        y_ref[s, :] = y
        send_ref[s, :] = y[:, :PASS]
        a, b, c, d = (got_ref[j, t, :].astype(F32) for j in range(4))
        grad_ref[s, :] = (cot_ref[s, :].astype(F32) + ((a + b) + (c + d))).astype(BF16)
    a, b, c, d = (got_ref[j, 2 * FX:, :].astype(F32) for j in range(4))
    line = jnp.sum((a + b) + (c + d), axis=0, keepdims=True)
    gain_grad_ref[...] = (line[:, :FX] / gain_ref[...].astype(F32)).reshape(FX)


def route_own(counts_ref, y_ref, out_ref, far_ref):
    rank = lax.axis_index(DP)
    counts = counts_ref[...]
    owners = lax.broadcasted_iota(jnp.int32, counts.shape, 1)
    live = jnp.sum(jnp.where(owners == rank, counts, 0), axis=1, keepdims=True) * WIN
    drift = drift_of(counts, rank) * WIN
    kept = W_DEV * WIN - drift
    r = lax.broadcasted_iota(jnp.int32, (ROWS, SLOTS), 0)
    c = lax.broadcasted_iota(jnp.int32, (ROWS, SLOTS), 1)
    own = jnp.where((r == c + drift) & (c < live), 1.0, 0.0).astype(BF16)
    out_ref[...] = dot(y_ref[...], own, (1, 0)).astype(BF16)
    r, c = r[:PASS], c[:PASS]
    far_ref[...] = jnp.where((r == c - kept) & (c < live), 1.0, 0.0).astype(BF16)


def route_far(own_ref, far_ref, got_ref, out_ref):
    out_ref[...] = (own_ref[...].astype(F32) + dot(got_ref[...], far_ref[...], (1, 0))).astype(BF16)


def shards(x_work, norm_gain, w_qkv, w_out, cot_owned, counts):
    xt, cot, wq = x_work.T, cot_owned.T, w_qkv.T
    counts = counts.reshape(1, -1)
    gain = norm_gain.reshape(1, -1)
    up = [(i, i + 1) for i in range(127)]
    down = [(i + 1, i) for i in range(127)]
    cores = [(0, 1), (1, 0)]

    got = lax.ppermute(cot, DP, up)
    x_full = lax.all_gather(xt, "x", axis=0, tiled=True)
    cot_work = call(
        route_in,
        struct((GROWS, ROWS), BF16),
        ins=(HBM, HBM, HBM, HBM),
        outs=HBM,
        scratch=(
            pltpu.VMEM((1, 128), jnp.int32),
            pltpu.VMEM((FX,), BF16),
            pltpu.VMEM((FX, ROWS), BF16),
            pltpu.VMEM((FX, SLOTS), BF16),
            pltpu.VMEM((GROWS, ROWS), BF16),
            pltpu.SemaphoreType.DMA((6,)),
        ),
        vmem_mib=61,
    )(counts, norm_gain, cot, got)
    g_full = lax.all_gather(cot_work, "x", axis=0)

    send, dsum, tile, gp, mx, gcol, rms = call(
        block,
        (
            struct((16, HALF + TILE), BF16),
            struct((QKV + ATT, FEAT), F32),
            struct((16, TILE), F32),
            struct((QKV, ROWS), BF16),
            struct((ATT, ROWS), BF16),
            struct((FEAT, 1), F32),
            struct((1, ROWS), F32),
        ),
        scratch=(
            pltpu.VMEM((FEAT, ROWS), BF16),
            pltpu.VMEM((FEAT, ROWS), BF16),
            pltpu.VMEM((QKV, ROWS), BF16),
            pltpu.VMEM((ATT, ROWS), BF16),
        ),
        vmem_mib=40,
        flops=1500000000,
    )(x_full, g_full, wq, w_out)

    got = lax.ppermute(send, "c", cores)
    heads_shape = struct((4, 2 * FX + 16, ROWS), BF16)
    heads = call(
        head_shares,
        heads_shape,
        outs=HBM,
        scratch=(
            pltpu.VMEM((FEAT, ROWS), F32),
            pltpu.VMEM((4, 2 * FX, ROWS), BF16),
            pltpu.SemaphoreType.DMA((4,)),
        ),
        vmem_mib=40,
        flops=700000000,
    )(gp, mx, x_full, wq, w_out, gcol, rms)

    parts = call(core_sum, struct((4, 16, Y_LANES + TILE), BF16))(dsum, tile, got)
    parts = lax.all_to_all(parts, "y", 0, 0)
    parts = call(y_sum, struct((4, 16, Z_LANES + TILE), BF16))(parts)
    parts = lax.all_to_all(parts, "zl", 0, 0)
    part = call(zl_sum, struct((16, Z_LANES + TILE), BF16))(parts)
    got = lax.ppermute(part, "zh", [(0, 1), (1, 0), (2, 3), (3, 2)])
    part = call(pair_sum, struct((16, Z_LANES + TILE), BF16), ins=(VMEM, VMEM, HBM))(part, got, heads)
    got = lax.ppermute(part, "zh", [(1, 2), (2, 1), (3, 0), (0, 3)])
    part, tile = call(zh_sum, (struct((16, Z_LANES), BF16), struct((16, TILE), F32)))(part, got)
    got = lax.ppermute(part, "zl", [(0, 3), (3, 0), (1, 2), (2, 1)])
    heads = call(
        gain_lines,
        heads_shape,
        ins=(VMEM, HBM),
        outs=HBM,
        aliases={1: 0},
        scratch=(pltpu.VMEM((4, 16, ROWS), BF16), pltpu.SemaphoreType.DMA((4,))),
    )(tile, heads)
    heads = lax.all_to_all(heads, "x", 0, 0)
    pair = call(z_pair, struct((2, 16, Z_LANES), BF16), flops=30000000000)(part, got)
    got = lax.ppermute(pair, "zl", [(0, 1), (1, 0), (2, 3), (3, 2)])
    part = call(z_pack, struct((16, Y_LANES), BF16))(pair, got)
    own = lax.all_gather(part, "y", axis=0)
    other = lax.ppermute(own, "c", cores)
    qkv_grad, out_grad = call(
        weights_out,
        (struct((QKV, FEAT), F32), struct((ATT, FEAT), F32)),
        ins=(VMEM, ANY),
        outs=(ANY, ANY),
        scratch=(
            pltpu.VMEM((4, 16, Y_LANES), BF16),
            pltpu.VMEM((QKV + ATT, FEAT), F32),
            pltpu.SemaphoreType.DMA((12,)),
        ),
    )(own, other)

    y_work, send, x_grad, gain_grad = call(
        heads_sum,
        (
            struct((FX, ROWS), BF16),
            struct((FX, PASS), BF16),
            struct((FX, ROWS), BF16),
            struct((FX,), F32),
        ),
    )(heads, xt, cot_work, gain)
    got = lax.ppermute(send, DP, down)
    own_slots, far = call(
        route_own,
        (struct((FX, SLOTS), BF16), struct((PASS, SLOTS), BF16)),
        flops=500000000,
    )(counts, y_work)
    y_owned = call(route_far, struct((FX, SLOTS), BF16))(own_slots, far, got)
    return (y_owned.T, x_grad.T, qkv_grad.T, out_grad, gain_grad)


def solution(mesh):
    fine = Mesh(mesh.devices.reshape(4, 4, 4, 2, 4), DP + ("x",))
    return jax.shard_map(
        shards,
        mesh=fine,
        in_specs=(P(DP, "x"), P("x"), P(None, "x"), P("x", None), P(DP, "x"), P()),
        out_specs=(P(DP, "x"), P(DP, "x"), P(None, "x"), P("x", None), P("x")),
        check_vma=False,
    )
```

```python
import jax
import jax.numpy as jnp
from jax import lax
from jax.experimental import pallas as pl
from jax.experimental.pallas import tpu as pltpu
from jax.sharding import Mesh, PartitionSpec as P

HD = 80
WIN = 64
W_DEV = 6
epsilon = 1e-06

F32 = jnp.float32
BF16 = jnp.bfloat16
DP = ("zh", "zl", "y", "c")

FEAT = 1280
ROWS = 384
FX = 320
QKV = 480
ATT = 160
HEADS = 2
SLOTS = 704
PASS = 320
GROWS = 336

HALF = 25600
Y_LANES = 6400
Z_LANES = 1664
TILE = 128

VMEM = pl.BlockSpec(memory_space=pltpu.VMEM)
ANY = pl.BlockSpec(memory_space=pl.ANY)
HBM = pl.BlockSpec(memory_space=pltpu.HBM)


def call(kernel, out_shapes, ins=None, outs=None, aliases=None, scratch=(), vmem_mib=24, flops=1000000):
    specs = {}
    if ins is not None:
        specs["in_specs"] = ins
    if outs is not None:
        specs["out_specs"] = outs
    return pl.pallas_call(
        kernel,
        out_shape=out_shapes,
        scratch_shapes=list(scratch),
        input_output_aliases=aliases or {},
        compiler_params=pltpu.CompilerParams(vmem_limit_bytes=vmem_mib * 1024 * 1024),
        cost_estimate=pl.CostEstimate(flops=flops, bytes_accessed=1000000, transcendentals=0),
        **specs,
    )


def struct(shape, dtype):
    return jax.ShapeDtypeStruct(shape, dtype)


def drift_of(counts_row, rank):
    owners = lax.broadcasted_iota(jnp.int32, counts_row.shape, 1)
    before = jnp.sum(jnp.where(owners < rank, counts_row, 0), axis=1, keepdims=True)
    return before - rank * W_DEV


def one_hot(rows, cols, shift):
    r = lax.broadcasted_iota(jnp.int32, (rows, cols), 0)
    c = lax.broadcasted_iota(jnp.int32, (rows, cols), 1)
    return jnp.where(r == c + shift, 1.0, 0.0).astype(BF16)


def dot(a, b, dims):
    return lax.dot_general(a, b, ((dims[:1], dims[1:]), ((), ())), preferred_element_type=F32)


def route_in(counts_hbm, gain_hbm, cot_hbm, got_hbm, out_hbm, counts, gain, cot, got, out, sems):
    loads = ((counts_hbm, counts), (gain_hbm, gain), (cot_hbm.at[:, pl.ds(0, ROWS)], cot), (got_hbm, got))
    loads = [pltpu.make_async_copy(a, b, sems.at[n]) for n, (a, b) in enumerate(loads)]
    for load in loads:
        load.start()
    loads[0].wait()
    rank = lax.axis_index(DP)
    drift = drift_of(counts[...], rank) * WIN
    drift_before = drift_of(counts[...], rank - 1) * WIN
    own = one_hot(ROWS, ROWS, -drift)
    col = lax.broadcasted_iota(jnp.int32, (SLOTS, ROWS), 1)
    row = lax.broadcasted_iota(jnp.int32, (SLOTS, ROWS), 0)
    near = jnp.where((row == col + (W_DEV * WIN - drift_before)) & (col < drift), 1.0, 0.0).astype(BF16)
    loads[1].wait()
    out[FX:, :] = jnp.zeros((GROWS - FX, ROWS), BF16)
    out[FX:, :FX] = jnp.broadcast_to(gain[...].reshape(1, FX), (GROWS - FX, FX))
    loads[2].wait()
    loads[3].wait()
    stores = []
    for n, (lo, hi) in enumerate(((0, 160), (160, FX))):
        block_rows = dot(cot[lo:hi, :], own, (1, 0)) + dot(got[lo:hi, :], near, (1, 0))
        out[lo:hi, :] = block_rows.astype(BF16)
        end = hi if n == 0 else GROWS
        rows = pl.ds(lo, end - lo)
        stores.append(pltpu.make_async_copy(out.at[rows], out_hbm.at[rows], sems.at[4 + n]))
        stores[n].start()
    for store in stores:
        store.wait()


def x_rows(x_ref, i):
    return x_ref[80 * i:80 * (i + 1), :]


def pairs():
    return [(3 * h + p, h, slice(128 * p, 128 * (p + 1)), 3 * HD * h) for h in range(HEADS) for p in range(3)]


def block(x_ref, g_ref, wq_ref, wo_ref, send_ref, dsum, tile_ref, gp_ref, mx_ref, gcol_ref, rms_ref, gt, nrm, pk, gm):
    core = lax.axis_index("c")
    r_i = lax.broadcasted_iota(jnp.int32, (FX, ROWS), 0)
    c_i = lax.broadcasted_iota(jnp.int32, (FX, ROWS), 1)
    total = jnp.zeros((8, ROWS), F32)
    for i in range(16):
        x = x_rows(x_ref, i).astype(F32)
        total += jnp.sum((x * x).reshape(10, 8, ROWS), axis=0)
    rms = lax.rsqrt(jnp.sum(total, axis=0, keepdims=True) / FEAT + epsilon)
    rms_ref[...] = rms
    for j in range(4):
        gt[FX * j:FX * (j + 1), :] = g_ref[j, :FX, :]
        row = g_ref[j, FX:, :].astype(F32)[:1, :]
        gcol_ref[FX * j:FX * (j + 1), :] = jnp.sum(jnp.where(r_i == c_i, row, 0.0), axis=1, keepdims=True)
    for i in range(16):
        s = slice(80 * i, 80 * (i + 1))
        nrm[s, :] = ((x_rows(x_ref, i).astype(F32) * rms) * gcol_ref[s, :]).astype(BF16)
    pk[...] = dot(wq_ref[...], nrm[...], (1, 0)).astype(BF16)
    gm[...] = dot(wo_ref[...], gt[...], (1, 0)).astype(BF16)
    qi = lax.broadcasted_iota(jnp.int32, (128, 128), 0)
    ki = lax.broadcasted_iota(jnp.int32, (128, 128), 1)
    same = (qi < WIN) == (ki < WIN)
    scores = [
        jnp.where(same, dot(pk[b:b + HD, c], pk[b + HD:b + 2 * HD, c], (0, 0)) * HD ** (-0.5), -jnp.inf)
        for _, _, c, b in pairs()
    ]
    dws = [dot(gm[HD * h:HD * (h + 1), c], pk[b + 2 * HD:b + 3 * HD, c], (0, 0)) for _, h, c, b in pairs()]
    exps = [jnp.exp(s - jnp.max(s, axis=1, keepdims=True)) for s in scores]
    probs = [e / jnp.sum(e, axis=1, keepdims=True) for e in exps]
    weights = [p.astype(BF16) for p in probs]
    dss = [
        (p * (dw - jnp.sum(dw * p, axis=1, keepdims=True)) * HD ** (-0.5)).astype(BF16)
        for p, dw in zip(probs, dws)
    ]
    for n, h, c, b in pairs():
        mx_ref[HD * h:HD * (h + 1), c] = dot(pk[b + 2 * HD:b + 3 * HD, c], weights[n], (1, 1)).astype(BF16)
        gp_ref[b:b + HD, c] = dot(pk[b + HD:b + 2 * HD, c], dss[n], (1, 1)).astype(BF16)
        gp_ref[b + HD:b + 2 * HD, c] = dot(pk[b:b + HD, c], dss[n], (1, 0)).astype(BF16)
        gp_ref[b + 2 * HD:b + 3 * HD, c] = dot(gm[HD * h:HD * (h + 1), c], weights[n], (1, 0)).astype(BF16)
    dsum[:QKV, :] = dot(gp_ref[...], nrm[...], (1, 1))
    dsum[QKV:, :] = dot(mx_ref[...], gt[...], (1, 1))
    for i in range(20):
        c = slice(FEAT * i, FEAT * (i + 1))
        send_ref[:, c] = dsum[pl.ds(pl.multiple_of((1 - core) * 320 + 16 * i, 16), 16), :].astype(BF16)
    total = jnp.zeros((8, FEAT), F32)
    for i in range(30):
        s = slice(16 * i, 16 * (i + 1))
        total += jnp.sum((wq_ref[s, :].astype(F32) * dsum[s, :]).reshape(2, 8, FEAT), axis=0)
    line = jnp.sum(total, axis=0, keepdims=True)
    tile_row = lax.broadcasted_iota(jnp.int32, (16, TILE), 0)
    tile = jnp.zeros((16, TILE), F32)
    for i in range(10):
        tile = jnp.where(tile_row == i, line[:, TILE * i:TILE * (i + 1)], tile)
    tile = tile.astype(BF16)
    send_ref[:, HALF:] = tile
    tile_ref[...] = tile.astype(F32)


def head_shares(gp_ref, mx_ref, x_ref, wq_ref, wo_ref, gcol_ref, rms_ref, heads_ref, part, out, sems):
    rms = rms_ref[...]
    part[...] = dot(wo_ref[...], mx_ref[...], (0, 0))
    for j in range(4):
        out[j, :FX, :] = part[FX * j:FX * (j + 1), :].astype(BF16)
    part[...] = dot(wq_ref[...], gp_ref[...], (0, 0))
    row_dot = jnp.zeros((8, ROWS), F32)
    for i in range(16):
        s = slice(80 * i, 80 * (i + 1))
        x = x_rows(x_ref, i).astype(F32)
        row_dot += jnp.sum(((part[s, :] * gcol_ref[s, :]) * (x * rms)).reshape(10, 8, ROWS), axis=0)
    mean = jnp.sum(row_dot, axis=0, keepdims=True) / FEAT
    copies = []
    for j in range(4):
        for i in range(4):
            s = slice(FX * j + 80 * i, FX * j + 80 * (i + 1))
            x = x_rows(x_ref, 4 * j + i).astype(F32)
            z = rms * (part[s, :] * gcol_ref[s, :] - (x * rms) * mean)
            out[j, FX + 80 * i:FX + 80 * (i + 1), :] = z.astype(BF16)
        copies.append(pltpu.make_async_copy(out.at[j], heads_ref.at[j, pl.ds(0, 2 * FX)], sems.at[j]))
        copies[j].start()
    for copy in copies:
        copy.wait()


def core_sum(dsum_ref, tile_ref, got_ref, out_ref):
    core = lax.axis_index("c")
    gain = (tile_ref[...] + got_ref[:, HALF:].astype(F32)).astype(BF16)
    for i in range(20):
        b, o = divmod(i, 5)
        own = dsum_ref[pl.ds(pl.multiple_of(core * 320 + 16 * i, 16), 16), :]
        got = got_ref[:, FEAT * i:FEAT * (i + 1)].astype(F32)
        out_ref[b, :, FEAT * o:FEAT * (o + 1)] = (own + got).astype(BF16)
    for b in range(4):
        out_ref[b, :, Y_LANES:] = gain


def sum_of_four(ref, s):
    a, b, c, d = (ref[i, :, s].astype(F32) for i in range(4))
    return (a + b) + (c + d)


def y_sum(got_ref, out_ref):
    gain = sum_of_four(got_ref, slice(Y_LANES, Y_LANES + TILE)).astype(BF16)
    for b in range(4):
        lo, hi = Z_LANES * b, min(Z_LANES * (b + 1), Y_LANES)
        out_ref[b, :, :hi - lo] = sum_of_four(got_ref, slice(lo, hi)).astype(BF16)
        if hi - lo < Z_LANES:
            out_ref[b, :, hi - lo:Z_LANES] = jnp.zeros((16, Z_LANES - (hi - lo)), BF16)
        out_ref[b, :, Z_LANES:] = gain


def zl_sum(got_ref, out_ref):
    out_ref[...] = sum_of_four(got_ref, slice(None)).astype(BF16)


def pair_sum(own_ref, got_ref, heads_ref, out_ref):
    out_ref[...] = (own_ref[...].astype(F32) + got_ref[...].astype(F32)).astype(BF16)


def zh_sum(own_ref, got_ref, out_ref, tile_ref):
    total = own_ref[...].astype(F32) + got_ref[...].astype(F32)
    out_ref[...] = total[:, :Z_LANES].astype(BF16)
    tile_ref[...] = total[:, Z_LANES:]


def gain_lines(tile_ref, heads_in, heads_ref, lines, sems):
    tile = tile_ref[...]
    line = jnp.concatenate([tile[i:i + 1, :] for i in range(10)], axis=1)
    row = lax.broadcasted_iota(jnp.int32, (16, FX), 0)
    copies = []
    for j in range(4):
        chunk = line[:, FX * j:FX * (j + 1)]
        high = chunk.astype(BF16).astype(F32)
        lines[j] = jnp.zeros((16, ROWS), BF16)
        lines[j, :, :FX] = jnp.where(row == 0, high, jnp.where(row == 1, chunk - high, 0.0)).astype(BF16)
        copies.append(pltpu.make_async_copy(lines.at[j], heads_ref.at[j, pl.ds(2 * FX, 16)], sems.at[j]))
        copies[j].start()
    for copy in copies:
        copy.wait()


def z_pair(own_ref, got_ref, out_ref):
    first = lax.axis_index("zl") < 2

    @pl.when(first)
    def _():
        out_ref[0] = own_ref[...]
        out_ref[1] = got_ref[...]

    @pl.when(jnp.logical_not(first))
    def _():
        out_ref[0] = got_ref[...]
        out_ref[1] = own_ref[...]


def z_pack(own_ref, got_ref, out_ref):
    zl = lax.axis_index("zl")
    outer = (zl == 0) | (zl == 3)

    def place(outer_ref, inner_ref):
        for n, shard in enumerate((outer_ref.at[0], inner_ref.at[0], inner_ref.at[1], outer_ref.at[1])):
            lo, hi = Z_LANES * n, min(Z_LANES * (n + 1), Y_LANES)
            out_ref[:, lo:hi] = shard[:, :hi - lo]

    @pl.when(outer)
    def _():
        place(own_ref, got_ref)

    @pl.when(jnp.logical_not(outer))
    def _():
        place(got_ref, own_ref)


def weights_out(own_ref, other_any, qkv_ref, out_ref, other, buf, sems):
    core = lax.axis_index("c")
    loads = [pltpu.make_async_copy(other_any.at[b], other.at[b], sems.at[8 + b]) for b in range(4)]
    for load in loads:
        load.start()
    for n in range(8):
        b = n % 4
        if n >= 4:
            loads[b].wait()
        ref, half = (own_ref, core) if n < 4 else (other, 1 - core)
        for o in range(5):
            row = 80 * n + 16 * o
            buf[row:row + 16, :] = ref[b, :, FEAT * o:FEAT * (o + 1)].astype(F32)
        chunk = buf.at[pl.ds(80 * n, 80)]

        @pl.when(half == 0)
        def _():
            pltpu.make_async_copy(chunk, qkv_ref.at[pl.ds(80 * b, 80)], sems.at[n]).start()

        @pl.when(half == 1)
        def _():
            target = qkv_ref.at[pl.ds(320 + 80 * b, 80)] if b < 2 else out_ref.at[pl.ds(80 * (b - 2), 80)]
            pltpu.make_async_copy(chunk, target, sems.at[n]).start()

    for n in range(8):
        pltpu.make_async_copy(buf.at[pl.ds(80 * n, 80)], qkv_ref.at[pl.ds(0, 80)], sems.at[n]).wait()


def y_heads(got_ref, x_ref, y_ref, send_ref):
    for i in range(5):
        s = slice(64 * i, 64 * (i + 1))
        a, b, c, d = (got_ref[j, s, :].astype(F32) for j in range(4))
        y = (x_ref[s, :].astype(F32) + ((a + b) + (c + d))).astype(BF16)
        y_ref[s, :] = y
        send_ref[s, :] = y[:, :PASS]


def x_heads(got_ref, cot_ref, gain_ref, grad_ref, gain_grad_ref):
    for i in range(5):
        s = slice(64 * i, 64 * (i + 1))
        a, b, c, d = (got_ref[j, FX + 64 * i:FX + 64 * (i + 1), :].astype(F32) for j in range(4))
        grad_ref[s, :] = (cot_ref[s, :].astype(F32) + ((a + b) + (c + d))).astype(BF16)
    a, b, c, d = (got_ref[j, 2 * FX:, :].astype(F32) for j in range(4))
    line = jnp.sum((a + b) + (c + d), axis=0, keepdims=True)
    gain_grad_ref[...] = (line[:, :FX] / gain_ref[...].astype(F32)).reshape(FX)


def route_own(counts_ref, y_ref, out_ref, far_ref):
    rank = lax.axis_index(DP)
    counts = counts_ref[...]
    owners = lax.broadcasted_iota(jnp.int32, counts.shape, 1)
    live = jnp.sum(jnp.where(owners == rank, counts, 0), axis=1, keepdims=True) * WIN
    drift = drift_of(counts, rank) * WIN
    kept = W_DEV * WIN - drift
    r = lax.broadcasted_iota(jnp.int32, (ROWS, SLOTS), 0)
    c = lax.broadcasted_iota(jnp.int32, (ROWS, SLOTS), 1)
    own = jnp.where((r == c + drift) & (c < live), 1.0, 0.0).astype(BF16)
    out_ref[...] = dot(y_ref[...], own, (1, 0)).astype(BF16)
    r, c = r[:PASS], c[:PASS]
    far_ref[...] = jnp.where((r == c - kept) & (c < live), 1.0, 0.0).astype(BF16)


def route_far(own_ref, far_ref, got_ref, out_ref):
    out_ref[...] = (own_ref[...].astype(F32) + dot(got_ref[...], far_ref[...], (1, 0))).astype(BF16)


def shards(x_work, norm_gain, w_qkv, w_out, cot_owned, counts):
    xt, cot, wq = x_work.T, cot_owned.T, w_qkv.T
    counts = counts.reshape(1, -1)
    gain = norm_gain.reshape(1, -1)
    up = [(i, i + 1) for i in range(127)]
    down = [(i + 1, i) for i in range(127)]
    cores = [(0, 1), (1, 0)]

    got = lax.ppermute(cot, DP, up)
    x_full = lax.all_gather(xt, "x", axis=0, tiled=True)
    cot_work = call(
        route_in,
        struct((GROWS, ROWS), BF16),
        ins=(HBM, HBM, HBM, HBM),
        outs=HBM,
        scratch=(
            pltpu.VMEM((1, 128), jnp.int32),
            pltpu.VMEM((FX,), BF16),
            pltpu.VMEM((FX, ROWS), BF16),
            pltpu.VMEM((FX, SLOTS), BF16),
            pltpu.VMEM((GROWS, ROWS), BF16),
            pltpu.SemaphoreType.DMA((6,)),
        ),
        vmem_mib=61,
    )(counts, norm_gain, cot, got)
    g_full = lax.all_gather(cot_work, "x", axis=0)

    send, dsum, tile, gp, mx, gcol, rms = call(
        block,
        (
            struct((16, HALF + TILE), BF16),
            struct((QKV + ATT, FEAT), F32),
            struct((16, TILE), F32),
            struct((QKV, ROWS), BF16),
            struct((ATT, ROWS), BF16),
            struct((FEAT, 1), F32),
            struct((1, ROWS), F32),
        ),
        scratch=(
            pltpu.VMEM((FEAT, ROWS), BF16),
            pltpu.VMEM((FEAT, ROWS), BF16),
            pltpu.VMEM((QKV, ROWS), BF16),
            pltpu.VMEM((ATT, ROWS), BF16),
        ),
        vmem_mib=40,
        flops=1500000000,
    )(x_full, g_full, wq, w_out)

    got = lax.ppermute(send, "c", cores)
    heads_shape = struct((4, 2 * FX + 16, ROWS), BF16)
    heads = call(
        head_shares,
        heads_shape,
        outs=HBM,
        scratch=(
            pltpu.VMEM((FEAT, ROWS), F32),
            pltpu.VMEM((4, 2 * FX, ROWS), BF16),
            pltpu.SemaphoreType.DMA((4,)),
        ),
        vmem_mib=40,
        flops=700000000,
    )(gp, mx, x_full, wq, w_out, gcol, rms)

    parts = call(core_sum, struct((4, 16, Y_LANES + TILE), BF16))(dsum, tile, got)
    parts = lax.all_to_all(parts, "y", 0, 0)
    parts = call(y_sum, struct((4, 16, Z_LANES + TILE), BF16))(parts)
    parts = lax.all_to_all(parts, "zl", 0, 0)
    part = call(zl_sum, struct((16, Z_LANES + TILE), BF16))(parts)
    got = lax.ppermute(part, "zh", [(0, 1), (1, 0), (2, 3), (3, 2)])
    part = call(pair_sum, struct((16, Z_LANES + TILE), BF16), ins=(VMEM, VMEM, HBM))(part, got, heads)
    got = lax.ppermute(part, "zh", [(1, 2), (2, 1), (3, 0), (0, 3)])
    part, tile = call(zh_sum, (struct((16, Z_LANES), BF16), struct((16, TILE), F32)))(part, got)
    got = lax.ppermute(part, "zl", [(0, 3), (3, 0), (1, 2), (2, 1)])
    heads = call(
        gain_lines,
        heads_shape,
        ins=(VMEM, HBM),
        outs=HBM,
        aliases={1: 0},
        scratch=(pltpu.VMEM((4, 16, ROWS), BF16), pltpu.SemaphoreType.DMA((4,))),
    )(tile, heads)
    heads = lax.all_to_all(heads, "x", 0, 0)
    pair = call(z_pair, struct((2, 16, Z_LANES), BF16), flops=30000000000)(part, got)
    got = lax.ppermute(pair, "zl", [(0, 1), (1, 0), (2, 3), (3, 2)])
    part = call(z_pack, struct((16, Y_LANES), BF16))(pair, got)
    own = lax.all_gather(part, "y", axis=0)
    other = lax.ppermute(own, "c", cores)
    qkv_grad, out_grad = call(
        weights_out,
        (struct((QKV, FEAT), F32), struct((ATT, FEAT), F32)),
        ins=(VMEM, ANY),
        outs=(ANY, ANY),
        scratch=(
            pltpu.VMEM((4, 16, Y_LANES), BF16),
            pltpu.VMEM((QKV + ATT, FEAT), F32),
            pltpu.SemaphoreType.DMA((12,)),
        ),
    )(own, other)

    y_work, send = call(y_heads, (struct((FX, ROWS), BF16), struct((FX, PASS), BF16)))(heads, xt)
    got = lax.ppermute(send, DP, down)
    x_grad, gain_grad = call(
        x_heads,
        (struct((FX, ROWS), BF16), struct((FX,), F32)),
        flops=500000000,
    )(heads, cot_work, gain)
    own_slots, far = call(
        route_own,
        (struct((FX, SLOTS), BF16), struct((PASS, SLOTS), BF16)),
        flops=500000000,
    )(counts, y_work)
    y_owned = call(route_far, struct((FX, SLOTS), BF16))(own_slots, far, got)
    return (y_owned.T, x_grad.T, qkv_grad.T, out_grad, gain_grad)


def solution(mesh):
    fine = Mesh(mesh.devices.reshape(4, 4, 4, 2, 4), DP + ("x",))
    return jax.shard_map(
        shards,
        mesh=fine,
        in_specs=(P(DP, "x"), P("x"), P(None, "x"), P("x", None), P(DP, "x"), P()),
        out_specs=(P(DP, "x"), P(DP, "x"), P(None, "x"), P("x", None), P("x")),
        check_vma=False,
    )
```
